32 devices in a mesh: dp: 4 (over y, x), seq: 8 (over z, core).
Axes of the slice: x: 2, y: 2, z: 4, core: 2. Of those that a mesh axis runs over, the one named last changes fastest.
Arguments:
- states: bfloat16 [4, 1024, 512], P('dp', 'seq'), may hold values from -6 to 6
- w_qkv: bfloat16 [512, 1536], replicated, may hold values from -0.25 to 0.25
- qv_bias: float32 [2, 512], replicated, may hold values from -2 to 2
- output_weight: bfloat16 [512, 512], replicated, may hold values from -1 to 1
- out_bias: float32 [512], replicated, may hold values from -2 to 2
- w_up: bfloat16 [512, 2048], replicated, may hold values from -0.25 to 0.25
- up_bias: float32 [2048], replicated, may hold values from -2 to 2
- w_down: bfloat16 [2048, 512], replicated, may hold values from -0.125 to 0.125
- down_bias: float32 [512], replicated, may hold values from -2 to 2
- norm_gain: float32 [2, 512], replicated, may hold values from 0.5 to 1.5
- norm_shift: float32 [2, 512], replicated, may hold values from -2 to 2
- halt_weight: float32 [512], replicated, may hold values from -0.25 to 0.25
- halt_bias: float32 [1], replicated, may hold values from -3 to 3
- cotangent: bfloat16 [4, 1024, 512], P('dp', 'seq'), may hold values from -6 to 6
- lengths: int32 [4], P('dp'), may hold values from 1 to 1024, as said below
- caps: int32 [4, 1024], P('dp', 'seq'), may hold values from 1 to 2
Outputs:
- final_state: float32 [4, 1024, 512], P('dp', 'seq')
- input_grad: float32 [4, 1024, 512], P('dp', 'seq')
- grad_w_qkv: float32 [512, 1536], replicated
- grad_qv_bias: float32 [2, 512], replicated
- grad_w_out: float32 [512, 512], replicated
- grad_out_bias: float32 [512], replicated
- grad_w_up: float32 [512, 2048], replicated
- grad_up_bias: float32 [2048], replicated
- grad_w_down: float32 [2048, 512], replicated
- grad_down_bias: float32 [512], replicated
- grad_norm_gain: float32 [2, 512], replicated
- grad_norm_shift: float32 [2, 512], replicated
- grad_halt_weight: float32 [512], replicated
- grad_halt_bias: float32 [1], replicated
The draws below stay inside these ranges and needn't reach their ends.
Inputs may be any that keep to these rules, and one draw needn't show every extreme that they name: `lengths`: of the 1 sequence of each index of dp, one has all 1024 positions valid.
All inputs are finite; a program needn't handle non-finite values.
Results may differ from the reference program's by a relative error of at most 0.033.
Values may be sent and summed in bfloat16 or wider, within the bound.
A program may use at most 192 MiB of HBM per device.

```python
import math
import jax
import jax.numpy as jnp
from jax import lax

D = 512
HEADS = 8
FF = 2048
PONDER = 2
SEQS_DEV = 1
SEQ_LEN = 1024
BATCH = 4
N_DP = 4


def draw_lengths(key, part):
    key = jax.random.fold_in(key, 7)
    seq_total = SEQS_DEV * N_DP
    drawn_lengths = jax.random.randint(jax.random.fold_in(key, 1), (seq_total,), 1, SEQ_LEN + 1)
    chosen = jax.random.randint(jax.random.fold_in(key, 2), (N_DP,), 0, SEQS_DEV)
    group_of = jnp.arange(seq_total) // SEQS_DEV
    member = jnp.arange(seq_total) % SEQS_DEV
    is_full = member == chosen[group_of]
    return jnp.where(is_full, SEQ_LEN, drawn_lengths).astype(jnp.int32)


def touch_ends(values, stream_key, least, top_value):
    spot = [jax.random.randint(jax.random.fold_in(stream_key, axis), (), 0, length) for axis, length in enumerate(values.shape)]
    main_axis = values.shape.index(max(values.shape))
    next_to = spot[:main_axis] + [(spot[main_axis] + 1) % values.shape[main_axis]] + spot[main_axis + 1:]
    return values.at[tuple(spot)].set(least).at[tuple(next_to)].set(top_value)


def block_scale(rng, shape, cuts, least, high):
    def one(dim, parts):
        steps = jax.random.uniform(jax.random.fold_in(jax.random.fold_in(rng, 6), dim), (parts,), jnp.float32, least / len(cuts), high / len(cuts))
        return jnp.repeat(jnp.exp(steps), shape[dim] // parts).reshape((-1,) + (1,) * (len(shape) - dim - 1))

    level = one(*cuts[0])
    for cut in cuts[1:]:
        level = level * one(*cut)
    return level


def normal_values(rng, shape, scale, most, cuts=(), kind=jnp.bfloat16):
    drawn = jax.random.normal(rng, shape, jnp.float32) * scale
    if len(cuts) > 0:
        drawn = block_scale(rng, shape, cuts, -0.22, 0.18) * drawn
    return jnp.clip(drawn, min=-most, max=most).astype(kind)


def setup_inputs(seed: int = 0) -> dict:
    keys = jax.random.split(jax.random.key(seed), 17)
    return {
        "states": normal_values(keys[0], (BATCH, SEQ_LEN, D), 1.0, 6.0, ((0, 4), (1, 8))),
        "w_qkv": normal_values(keys[1], (D, 3 * D), D ** -0.5, 0.25),
        "qv_bias": normal_values(keys[2], (2, D), 0.3, 2.0, (), jnp.float32),
        "output_weight": normal_values(keys[3], (D, D), (D // 16) ** -0.5, 1.0),
        "out_bias": normal_values(keys[4], (D,), 0.3, 2.0, (), jnp.float32),
        "w_up": normal_values(keys[5], (D, FF), D ** -0.5, 0.25),
        "up_bias": normal_values(keys[6], (FF,), 0.3, 2.0, (), jnp.float32),
        "w_down": normal_values(keys[7], (FF, D), FF ** -0.5, 0.125),
        "down_bias": normal_values(keys[8], (D,), 0.3, 2.0, (), jnp.float32),
        "norm_gain": jnp.clip(1.0 + 0.1 * jax.random.normal(keys[9], (2, D), jnp.float32), 0.5, 1.5),
        "norm_shift": normal_values(keys[10], (2, D), 0.3, 2.0, (), jnp.float32),
        "halt_weight": normal_values(keys[11], (D,), D ** -0.5, 0.25, (), jnp.float32),
        "halt_bias": normal_values(keys[12], (1,), 1.0, 3.0, (), jnp.float32),
        "cotangent": normal_values(keys[13], (BATCH, SEQ_LEN, D), 1.0, 6.0, ((0, 4), (1, 8))),
        "lengths": draw_lengths(jax.random.fold_in(keys[16], 71), 0),
        "caps": touch_ends(jax.random.randint(keys[15], (BATCH, SEQ_LEN), 1, PONDER + 1), jax.random.fold_in(keys[15], 1), 1, PONDER).astype(jnp.int32),
    }


PONDER_COST = 0.01
NORM_EPSILON = 1e-05
MASK_FILL = -1e+30
BEST_PRECISION = lax.Precision.HIGHEST

@jax.custom_vjp
def low(v):
    return lax.optimization_barrier(v.astype(jnp.bfloat16)).astype(jnp.float32)

@jax.custom_vjp
def low_back(v):
    return v

def low_keep(v):
    return (low(v), None)

def low_pass(kept, grad):
    return (grad,)

def back_keep(v):
    return (v, None)

def back_low(kept, grad):
    return (low(grad),)
low.defvjp(low_keep, low_pass)
low_back.defvjp(back_keep, back_low)

def normalize(resid, gain, shift):
    centered = resid - lax.optimization_barrier(jnp.mean(resid, axis=-1, keepdims=True))
    spread = lax.optimization_barrier(jnp.mean(centered * centered, axis=-1, keepdims=True))
    return centered * lax.rsqrt(spread + NORM_EPSILON) * gain + shift

def halt_mix(halt_probs, caps):
    step_count = halt_probs.shape[-1] + 1
    remain = jnp.ones(caps.shape, halt_probs.dtype)
    leftover = jnp.zeros(caps.shape, halt_probs.dtype)
    columns = []
    for number in range(step_count):
        if number < step_count - 1:
            partial_weight = halt_probs[..., number] * remain
        else:
            partial_weight = jnp.zeros(caps.shape, halt_probs.dtype)
        column = jnp.where(caps > number + 1, partial_weight, jnp.where(caps == number + 1, remain, 0.0))
        columns.append(column)
        leftover = jnp.where(caps == number + 1, remain, leftover)
        if number < step_count - 1:
            remain = remain * (1.0 - halt_probs[..., number])
    return (jnp.stack(columns, -1), leftover)

def attend_sequence(inputs):
    queries, key_rows, value_rows, length = inputs
    seq_len = queries.shape[0]
    block_len = math.gcd(seq_len, 512)
    key_valid = jnp.arange(seq_len) < length
    score_scale = queries.shape[-1] ** (-0.5)

    def query_block(block_queries):
        scores = low_back(jnp.einsum('qhe,khe->hqk', block_queries, key_rows, precision=BEST_PRECISION) * score_scale)
        scores = jnp.where(key_valid[None, None, :], scores, MASK_FILL)
        row_max = lax.optimization_barrier(jnp.max(scores, axis=-1, keepdims=True))
        unnormed = jnp.where(key_valid[None, None, :], jnp.exp(scores - row_max), 0.0)
        probs_low = low(unnormed / lax.optimization_barrier(jnp.sum(unnormed, axis=-1, keepdims=True)))
        return jnp.einsum('hqk,khe->qhe', probs_low, value_rows, precision=BEST_PRECISION)
    blocks = queries.reshape(seq_len // block_len, block_len, queries.shape[1], queries.shape[2])
    context = lax.map(jax.checkpoint(query_block), blocks)
    return context.reshape(queries.shape)

def ponder_block(current, weights_tuple, lengths):
    w_qkv, qv_bias, output_weight, out_bias, w_up, up_bias, w_down, down_bias, norm_gain, norm_shift = weights_tuple
    seq_total, seq_len, model_width = current.shape
    rounded = low(current)
    projected = jnp.einsum('bld,df->blf', rounded, w_qkv, precision=BEST_PRECISION)
    queries = low(low_back(projected[..., :model_width] + qv_bias[0]))
    key_rows = low(low_back(projected[..., model_width:2 * model_width]))
    value_rows = low(low_back(projected[..., 2 * model_width:] + qv_bias[1]))
    split_shape = (seq_total, seq_len, HEADS, model_width // HEADS)
    context = lax.map(jax.checkpoint(attend_sequence), (queries.reshape(split_shape), key_rows.reshape(split_shape), value_rows.reshape(split_shape), lengths))
    context_reduced = low(low_back(context.reshape(current.shape)))
    attended = low_back(jnp.einsum('bld,de->ble', context_reduced, output_weight, precision=BEST_PRECISION) + out_bias)
    normed_one = normalize(current + attended, norm_gain[0], norm_shift[0])
    pre_hidden = low_back(jnp.einsum('bld,df->blf', low(normed_one), w_up, precision=BEST_PRECISION) + up_bias)
    hidden_low = low(jax.nn.gelu(pre_hidden))
    mlp_out = low_back(jnp.einsum('blf,fd->bld', hidden_low, w_down, precision=BEST_PRECISION) + down_bias)
    return normalize(normed_one + mlp_out, norm_gain[1], norm_shift[1])

def reference(states, w_qkv, qv_bias, output_weight, out_bias, w_up, up_bias, w_down, down_bias, norm_gain, norm_shift, halt_weight, halt_bias, cotangent, lengths, caps):

    def forward(current, p_qkv, p_qv_bias, p_out, p_out_bias, p_up, p_up_bias, p_down, p_down_bias, p_gain, p_shift, p_halt_weight, p_halt_bias):
        weights_tuple = (p_qkv, p_qv_bias, p_out, p_out_bias, p_up, p_up_bias, p_down, p_down_bias, p_gain, p_shift)
        history = []
        prob_list = []
        for number in range(PONDER):
            if number < PONDER - 1:
                prob_list.append(jax.nn.sigmoid(lax.optimization_barrier(jnp.sum(current * p_halt_weight, axis=-1)) + p_halt_bias[0]))
            updated = ponder_block(current, weights_tuple, lengths)
            current = jnp.where((caps > number)[..., None], updated, current)
            history.append(current)
        mixing, leftover = halt_mix(jnp.stack(prob_list, -1), caps)
        final_state = jnp.zeros_like(current)
        for number in range(PONDER):
            final_state = final_state + mixing[..., number, None] * history[number]
        return (final_state, jnp.sum(leftover))
    primals = (states.astype(jnp.float32), w_qkv.astype(jnp.float32), qv_bias, output_weight.astype(jnp.float32), out_bias, w_up.astype(jnp.float32), up_bias, w_down.astype(jnp.float32), down_bias, norm_gain, norm_shift, halt_weight, halt_bias)
    outputs, pull = jax.vjp(forward, *primals)
    grads = pull((cotangent.astype(jnp.float32), jnp.asarray(PONDER_COST, outputs[1].dtype)))
    return (outputs[0], grads[0], grads[1], grads[2], grads[3], grads[4], grads[5], grads[6], grads[7], grads[8], grads[9], grads[10], grads[11], grads[12])
```

```python
import math

import jax
import jax.numpy as jnp
from jax import lax
from jax.experimental import pallas as pl
from jax.experimental.pallas import tpu as pltpu
from jax.sharding import PartitionSpec as P

HEADS = 8
PONDER = 2


PONDER_COST = 0.01
NORM_EPSILON = 1e-05
MASK_FILL = -1e30


def normalize(resid, gain, shift):
    centered = resid - jnp.mean(resid, axis=-1, keepdims=True)
    spread = jnp.mean(centered * centered, axis=-1, keepdims=True)
    return centered * lax.rsqrt(spread + NORM_EPSILON) * gain + shift


def halt_mix(halt_probs, caps):
    step_count = halt_probs.shape[-1] + 1
    remain = jnp.ones(caps.shape, halt_probs.dtype)
    leftover = jnp.zeros(caps.shape, halt_probs.dtype)
    columns = []
    for number in range(step_count):
        if number < step_count - 1:
            partial_weight = halt_probs[..., number] * remain
        else:
            partial_weight = jnp.zeros(caps.shape, halt_probs.dtype)
        column = jnp.where(
            caps > number + 1, partial_weight, jnp.where(caps == number + 1, remain, 0.0)
        )
        columns.append(column)
        leftover = jnp.where(caps == number + 1, remain, leftover)
        if number < step_count - 1:
            remain = remain * (1.0 - halt_probs[..., number])
    return (jnp.stack(columns, -1), leftover)


def block_of_heads(piece_rows, offset_rows, block_len, head_count):
    sliced = lax.dynamic_slice_in_dim(piece_rows, offset_rows, block_len, 1)
    return sliced.reshape(sliced.shape[0], block_len, head_count, sliced.shape[2] // head_count)


def key_mask(lengths, offset_rows, block_len):
    positions = offset_rows + jnp.arange(block_len, dtype=jnp.int32)
    return (positions[None, :] < lengths[:, None])[:, None, None, :]


def attend(queries, key_rows, value_rows, lengths, head_count):
    seq_count, shard_len, model_width = queries.shape
    head_size = model_width // head_count
    score_scale = head_size ** (-0.5)
    query_heads = queries.reshape(seq_count, shard_len, head_count, head_size)
    start_state = (
        jnp.full((seq_count, head_count, shard_len), MASK_FILL, jnp.float32),
        jnp.zeros((seq_count, head_count, shard_len), jnp.float32),
        jnp.zeros((seq_count, shard_len, head_count, head_size), jnp.float32),
    )
    key_piece = lax.all_gather(key_rows, "seq", axis=1, tiled=True)
    value_piece = lax.all_gather(value_rows, "seq", axis=1, tiled=True)
    row_count = key_piece.shape[1]
    block_len = math.gcd(row_count, 512)

    def one_block(block_index, inner):
        running_max, running_sum, weighted = inner
        offset_rows = block_index * block_len
        key_block = block_of_heads(key_piece, offset_rows, block_len, head_count)
        value_block = block_of_heads(value_piece, offset_rows, block_len, head_count)
        key_valid = key_mask(lengths, offset_rows, block_len)
        scores = (
            jnp.einsum(
                "sqhe,skhe->shqk", query_heads, key_block, preferred_element_type=jnp.float32
            )
            * score_scale
        )
        scores = jnp.where(key_valid, scores, MASK_FILL)
        new_max = jnp.maximum(running_max, jnp.max(scores, axis=-1))
        unnormed = jnp.where(key_valid, jnp.exp(scores - new_max[..., None]), 0.0)
        factor = jnp.exp(running_max - new_max)
        running_sum = running_sum * factor + jnp.sum(unnormed, axis=-1)
        update = jnp.einsum(
            "shqk,skhe->sqhe",
            unnormed.astype(jnp.bfloat16),
            value_block,
            preferred_element_type=jnp.float32,
        )
        weighted = weighted * jnp.transpose(factor, (0, 2, 1))[..., None] + update
        return (new_max, running_sum, weighted)

    running_max, running_sum, weighted = lax.fori_loop(
        0, row_count // block_len, one_block, start_state
    )
    context = (weighted / jnp.transpose(running_sum, (0, 2, 1))[..., None]).reshape(queries.shape)
    log_total = jnp.transpose(running_max + jnp.log(running_sum), (0, 2, 1))
    return (context, log_total)


def attend_back(
    queries, key_rows, value_rows, lengths, head_count, grad_context, context, log_total
):
    seq_count, shard_len, model_width = queries.shape
    head_size = model_width // head_count
    score_scale = head_size ** (-0.5)
    query_heads = queries.reshape(seq_count, shard_len, head_count, head_size)
    grad_heads = grad_context.reshape(seq_count, shard_len, head_count, head_size)
    row_dots = jnp.sum(
        grad_context.astype(jnp.float32).reshape(grad_heads.shape)
        * context.reshape(grad_heads.shape),
        axis=-1,
    )
    dots_heads = jnp.transpose(row_dots, (0, 2, 1))
    log_heads = jnp.transpose(log_total, (0, 2, 1))
    total_len = shard_len * lax.axis_size("seq")
    start_state = (
        jnp.zeros(query_heads.shape, jnp.float32),
        jnp.zeros((seq_count, total_len, model_width), jnp.float32),
        jnp.zeros((seq_count, total_len, model_width), jnp.float32),
    )
    key_piece = lax.all_gather(key_rows, "seq", axis=1, tiled=True)
    value_piece = lax.all_gather(value_rows, "seq", axis=1, tiled=True)
    row_count = key_piece.shape[1]
    block_len = math.gcd(row_count, 512)

    def one_block(block_index, inner):
        grad_query, grad_key_all, grad_value_all = inner
        offset_rows = block_index * block_len
        key_block = block_of_heads(key_piece, offset_rows, block_len, head_count)
        value_block = block_of_heads(value_piece, offset_rows, block_len, head_count)
        key_valid = key_mask(lengths, offset_rows, block_len)
        scores = (
            jnp.einsum(
                "sqhe,skhe->shqk", query_heads, key_block, preferred_element_type=jnp.float32
            )
            * score_scale
        )
        probs = jnp.where(key_valid, jnp.exp(scores - log_heads[..., None]), 0.0)
        grad_probs = jnp.einsum(
            "sqhe,skhe->shqk", grad_heads, value_block, preferred_element_type=jnp.float32
        )
        grad_scores = (probs * (grad_probs - dots_heads[..., None])).astype(jnp.bfloat16)
        grad_query = grad_query + score_scale * jnp.einsum(
            "shqk,skhe->sqhe", grad_scores, key_block, preferred_element_type=jnp.float32
        )
        key_part = score_scale * jnp.einsum(
            "shqk,sqhe->skhe", grad_scores, query_heads, preferred_element_type=jnp.float32
        )
        value_part = jnp.einsum(
            "shqk,sqhe->skhe",
            probs.astype(jnp.bfloat16),
            grad_heads,
            preferred_element_type=jnp.float32,
        )
        grad_key_all = lax.dynamic_update_slice_in_dim(
            grad_key_all, key_part.reshape(seq_count, block_len, model_width), offset_rows, 1
        )
        grad_value_all = lax.dynamic_update_slice_in_dim(
            grad_value_all, value_part.reshape(seq_count, block_len, model_width), offset_rows, 1
        )
        return (grad_query, grad_key_all, grad_value_all)

    grad_query, grad_key_all, grad_value_all = lax.fori_loop(
        0, row_count // block_len, one_block, start_state
    )
    grad_key, grad_value = (
        lax.psum_scatter(grad_key_all, "seq", scatter_dimension=1, tiled=True),
        lax.psum_scatter(grad_value_all, "seq", scatter_dimension=1, tiled=True),
    )
    return (grad_query.reshape(queries.shape), grad_key, grad_value)


def forward_block(current, weights_tuple, lengths, head_count):
    (
        w_qkv,
        qv_bias,
        output_weight,
        out_bias,
        w_up,
        up_bias,
        w_down,
        down_bias,
        norm_gain,
        norm_shift,
    ) = weights_tuple
    model_width = current.shape[-1]
    rounded = current.astype(jnp.bfloat16)
    projected = jnp.einsum("snd,df->snf", rounded, w_qkv, preferred_element_type=jnp.float32)
    queries = (projected[..., :model_width] + qv_bias[0]).astype(jnp.bfloat16)
    key_rows = projected[..., model_width : 2 * model_width].astype(jnp.bfloat16)
    value_rows = (projected[..., 2 * model_width :] + qv_bias[1]).astype(jnp.bfloat16)
    context, log_total = attend(queries, key_rows, value_rows, lengths, head_count)
    context_reduced = context.astype(jnp.bfloat16)
    resid_one = (
        current
        + jnp.einsum(
            "jry,ym->jrm", context_reduced, output_weight, preferred_element_type=jnp.float32
        )
        + out_bias
    )
    normed_one = normalize(resid_one, norm_gain[0], norm_shift[0])
    normed_low = normed_one.astype(jnp.bfloat16)
    pre_hidden = (
        jnp.einsum("snd,df->snf", normed_low, w_up, preferred_element_type=jnp.float32) + up_bias
    )
    hidden_low = jax.nn.gelu(pre_hidden).astype(jnp.bfloat16)
    resid_two = (
        normed_one
        + jnp.einsum("snf,fd->snd", hidden_low, w_down, preferred_element_type=jnp.float32)
        + down_bias
    )
    updated = normalize(resid_two, norm_gain[1], norm_shift[1])
    return {
        "rounded": rounded,
        "queries": queries,
        "key_rows": key_rows,
        "value_rows": value_rows,
        "context": context,
        "log_total": log_total,
        "context_low": context_reduced,
        "resid_one": resid_one,
        "normed_low": normed_low,
        "pre_hidden": pre_hidden,
        "hidden_low": hidden_low,
        "resid_two": resid_two,
        "updated": updated,
    }


def backward_block(grad_updated, saved_entry, weights_tuple, lengths, head_count):
    (
        w_qkv,
        qv_bias,
        output_weight,
        out_bias,
        w_up,
        up_bias,
        w_down,
        down_bias,
        norm_gain,
        norm_shift,
    ) = weights_tuple
    model_width = output_weight.shape[0]
    _, pull_two = jax.vjp(normalize, saved_entry["resid_two"], norm_gain[1], norm_shift[1])
    grad_resid_two, gain_two, shift_two = pull_two(grad_updated)
    grad_mlp = grad_resid_two.astype(jnp.bfloat16)
    grad_down_bias = jnp.sum(grad_mlp.astype(jnp.float32), axis=(0, 1))
    grad_w_down = jnp.einsum(
        "snf,snd->fd", saved_entry["hidden_low"], grad_mlp, preferred_element_type=jnp.float32
    )
    grad_hidden = jnp.einsum("snd,fd->snf", grad_mlp, w_down, preferred_element_type=jnp.float32)
    _, pull_gelu = jax.vjp(jax.nn.gelu, saved_entry["pre_hidden"])
    grad_pre = pull_gelu(grad_hidden)[0].astype(jnp.bfloat16)
    grad_up_bias = jnp.sum(grad_pre.astype(jnp.float32), axis=(0, 1))
    grad_w_up = jnp.einsum(
        "snd,snf->df", saved_entry["normed_low"], grad_pre, preferred_element_type=jnp.float32
    )
    grad_normed = grad_resid_two + jnp.einsum(
        "snf,df->snd", grad_pre, w_up, preferred_element_type=jnp.float32
    )
    _, pull_one = jax.vjp(normalize, saved_entry["resid_one"], norm_gain[0], norm_shift[0])
    grad_resid_one, gain_one, shift_one = pull_one(grad_normed)
    attended_gradient = grad_resid_one.astype(jnp.bfloat16)
    grad_out_bias = jnp.sum(attended_gradient.astype(jnp.float32), axis=(0, 1))
    grad_w_out = jnp.einsum(
        "jhv,jhp->vp",
        saved_entry["context_low"],
        attended_gradient,
        preferred_element_type=jnp.float32,
    )
    grad_context = jnp.einsum(
        "yjo,io->yji", attended_gradient, output_weight, preferred_element_type=jnp.float32
    ).astype(jnp.bfloat16)
    grad_query, grad_key, grad_value = attend_back(
        saved_entry["queries"],
        saved_entry["key_rows"],
        saved_entry["value_rows"],
        lengths,
        head_count,
        grad_context,
        saved_entry["context"],
        saved_entry["log_total"],
    )
    grad_mixed = jnp.concatenate(
        [
            grad_query.astype(jnp.bfloat16),
            grad_key.astype(jnp.bfloat16),
            grad_value.astype(jnp.bfloat16),
        ],
        axis=-1,
    )
    grad_qv_bias = jnp.stack(
        [
            jnp.sum(grad_mixed[..., :model_width].astype(jnp.float32), axis=(0, 1)),
            jnp.sum(grad_mixed[..., 2 * model_width :].astype(jnp.float32), axis=(0, 1)),
        ]
    )
    grad_w_qkv = jnp.einsum(
        "snd,snf->df", saved_entry["rounded"], grad_mixed, preferred_element_type=jnp.float32
    )
    grad_current = grad_resid_one + jnp.einsum(
        "snf,df->snd", grad_mixed, w_qkv, preferred_element_type=jnp.float32
    )
    return (
        grad_current,
        (
            grad_w_qkv,
            grad_qv_bias,
            grad_w_out,
            grad_out_bias,
            grad_w_up,
            grad_up_bias,
            grad_w_down,
            grad_down_bias,
            jnp.stack([gain_one, gain_two]),
            jnp.stack([shift_one, shift_two]),
        ),
    )


def local(
    states,
    w_qkv,
    qv_bias,
    output_weight,
    out_bias,
    w_up,
    up_bias,
    w_down,
    down_bias,
    norm_gain,
    norm_shift,
    halt_weight,
    halt_bias,
    cotangent,
    lengths,
    caps,
):
    weights_tuple = (
        w_qkv,
        qv_bias,
        output_weight,
        out_bias,
        w_up,
        up_bias,
        w_down,
        down_bias,
        norm_gain,
        norm_shift,
    )
    head_count = HEADS
    current = states.astype(jnp.float32)
    inputs = []
    history = []
    prob_list = []
    for number in range(PONDER):
        if number < PONDER - 1:
            prob_list.append(jax.nn.sigmoid(jnp.sum(current * halt_weight, axis=-1) + halt_bias[0]))
        saved_entry = forward_block(current, weights_tuple, lengths, head_count)
        inputs.append(current)
        current = jnp.where((caps > number)[..., None], saved_entry["updated"], current)
        history.append(current)
    halt_probs = jnp.stack(prob_list, -1)
    (mixing, leftover), pull_halt = jax.vjp(lambda probs_in: halt_mix(probs_in, caps), halt_probs)
    final_state = jnp.zeros_like(current)
    for number in range(PONDER):
        final_state = final_state + mixing[..., number, None] * history[number]
    out_grad = cotangent.astype(jnp.float32)
    grad_mixing = jnp.stack(
        [jnp.sum(out_grad * history[number], axis=-1) for number in range(PONDER)], -1
    )
    grad_probs = pull_halt((grad_mixing, jnp.full(leftover.shape, PONDER_COST, jnp.float32)))[0]
    logits_gradient = grad_probs * halt_probs * (1.0 - halt_probs)
    totals = None
    grad_halt_weight = jnp.zeros(halt_weight.shape, jnp.float32)
    grad_halt_bias = jnp.zeros(halt_bias.shape, jnp.float32)
    grad_state = jnp.zeros(current.shape, jnp.float32)
    for number in reversed(range(PONDER)):
        grad_state = grad_state + out_grad * mixing[..., number, None]
        active = (caps > number)[..., None]
        grad_updated = jnp.where(active, grad_state, 0.0)
        passed = jnp.where(active, 0.0, grad_state)
        saved_entry = forward_block(inputs[number], weights_tuple, lengths, head_count)
        grad_prev, param_grads = backward_block(
            grad_updated, saved_entry, weights_tuple, lengths, head_count
        )
        totals = param_grads if totals is None else jax.tree.map(jnp.add, totals, param_grads)
        grad_state = passed + grad_prev
        if number < PONDER - 1:
            logit_grad = logits_gradient[..., number]
            grad_state = grad_state + logit_grad[..., None] * halt_weight
            grad_halt_weight = jnp.sum(logit_grad[..., None] * inputs[number], axis=(0, 1))
            grad_halt_bias = jnp.sum(logit_grad).reshape(1)
    summed = lax.psum(
        (
            totals[0],
            totals[1],
            totals[2],
            totals[3],
            totals[4],
            totals[5],
            totals[6],
            totals[7],
            totals[8],
            totals[9],
            grad_halt_weight,
            grad_halt_bias,
        ),
        ("dp", "seq"),
    )
    return (final_state, grad_state) + tuple(summed)


BF = jnp.bfloat16
F32 = jnp.float32
MESH = pl.DeviceIdType.MESH
GELU_A = math.sqrt(2.0 / math.pi)
GELU_B = 0.044715


def nn(a, b):
    return lax.dot_general(a, b, (((1,), (0,)), ((), ())), preferred_element_type=F32)


def nt(a, b):
    return lax.dot_general(a, b, (((1,), (1,)), ((), ())), preferred_element_type=F32)


def tn(a, b):
    return lax.dot_general(a, b, (((0,), (0,)), ((), ())), preferred_element_type=F32)


def colsum(v):
    return jnp.sum(v, axis=0, keepdims=True)


def rowsum(v):
    return jnp.sum(v, axis=1, keepdims=True)


class Links:
    def __init__(self, send, recv):
        self.send, self.recv, self.used, self.open = send, recv, 0, []

    def copy(self, src, dst, device):
        at = self.used
        self.used += 1
        made = pltpu.make_async_remote_copy(
            src_ref=src,
            dst_ref=dst,
            send_sem=self.send.at[at],
            recv_sem=self.recv.at[at],
            device_id=device,
            device_id_type=MESH,
        )
        return made

    def start(self, src, dst, device):
        made = self.copy(src, dst, device)
        made.start()
        self.open.append(made)
        return made

    def drain(self):
        for made in self.open:
            made.wait_send()
        self.open = []


N_LINKS = 160
TOK = 128
ROWS = 256
WIDE = 512
HALF = 1024
FEAT = 256
HEADC = 4
KEYS = 256
SLOTS = 4
QROWS = HEADC * ROWS
CHUNK = 128


def fused_kernel(
    states, cot_in, aux_in, vec, wqkv_all, wout_all, wup_all, wdown_all,
    final_out, igrad_out, small_out, gqkv_out, gout_out, gup_out, gdown_out,
    send_sem, recv_sem, local_sem,
    wqkv, wout, wup, wdown,
    st, ct, ax,
    s, rnd, q4, kv, ctxt, ctxlt, x1, rs1, n1low, hid, dgelu, x2, rs2, logt,
    scores, dprobs, probs, dsc, mrow, lrow, part_ctx, drow, do4,
    xch, xrecv, gcur, gres, dqt, dkv_own, dkv_send, dkv_recv, dqkv, small,
    gdown, gup, gqkv, gout,
    sa_all, ra_all, sb_all, rb_all, sc_all, rc_all, u_all, out_all,
    smallx, fin_t, ig_t,
):
    dp = lax.axis_index("dp")
    sq = lax.axis_index("seq")
    x, y = lax.rem(dp, 2), dp // 2
    z, c = sq // 2, lax.rem(sq, 2)

    def flip(value, bit):
        return value + bit - 2 * bit * lax.rem(value // bit, 2)

    sib = (dp, flip(sq, 1))
    to_x = (flip(dp, 1), sq)
    to_y = (flip(dp, 2), sq)
    z1 = (dp, flip(sq, 2))
    z2 = (dp, flip(sq, 4))
    z3 = (dp, flip(flip(sq, 2), 4))
    diag = (flip(dp, 1), flip(sq, 2))
    swap = (flip(dp, 1), flip(sq, 4))
    peers = (sib, to_x, to_y, z1, z2, z3, diag, swap)

    loads = []

    def load(src, dst):
        made = pltpu.make_async_copy(src, dst, local_sem.at[len(loads)])
        made.start()
        loads.append(made)

    own = pl.multiple_of(c * FEAT, FEAT)
    for third in range(3):
        load(
            wqkv_all.at[:, pl.ds(pl.multiple_of(third * WIDE + own, FEAT), FEAT)],
            wqkv.at[:, pl.ds(third * FEAT, FEAT)],
        )
    load(wout_all.at[pl.ds(own, FEAT), :], wout)
    wide_own = pl.multiple_of(c * HALF, HALF)
    load(wup_all.at[:, pl.ds(wide_own, HALF)], wup)
    load(wdown_all.at[pl.ds(wide_own, HALF), :], wdown)

    barrier = pltpu.get_barrier_semaphore()
    for peer in peers:
        pl.semaphore_signal(barrier, inc=1, device_id=peer, device_id_type=MESH)
    pl.semaphore_wait(barrier, len(peers))

    links = Links(send_sem, recv_sem)

    moved = x != z // 2
    swaps = [
        links.copy(states, st.at[c], swap),
        links.copy(aux_in, ax.at[c], swap),
        links.copy(cot_in, ct.at[c], swap),
    ]

    @pl.when(moved)
    def _():
        for made in swaps:
            made.start()
        swaps[0].wait_recv()
        swaps[1].wait_recv()

    @pl.when(jnp.logical_not(moved))
    def _():
        st[c] = states[...]
        ax[c] = aux_in[...]
        ct[c] = cot_in[...]

    pair_st = links.start(st.at[c], st.at[c], sib)
    pair_ax = links.start(ax.at[c], ax.at[c], sib)
    pair_st.wait_recv()
    pair_ax.wait_recv()

    caps = ax[...].reshape(ROWS, 128)[:, 0:1]
    length = ax[0, 0:1, 1:2]
    def block_of(xx, zz):
        return jnp.where(xx == zz // 2, zz, flip(zz, 2))

    zf, xf = flip(z, 1), 1 - x
    places = (block_of(x, z), block_of(xf, z), block_of(x, zf), block_of(xf, zf))
    key_iota = lax.broadcasted_iota(jnp.int32, (KEYS, 1), 0)
    biases = []
    for place in places:
        positions = (key_iota + place * KEYS).astype(F32)
        biases.append(jnp.where(positions < length, 0.0, MASK_FILL))

    row = lambda i: vec[i : i + 1, :]
    mine = lambda v: jnp.where(c == 0, v[:, :FEAT], v[:, FEAT:])
    bias_q, bias_v = mine(row(0)), mine(row(1))
    up_bias = jnp.concatenate(
        [jnp.where(c == 0, row(3), row(5)), jnp.where(c == 0, row(4), row(6))], axis=1
    )
    lane_head = lax.broadcasted_iota(jnp.int32, (1, FEAT), 1) // 64

    s[0] = st[...].reshape(ROWS, WIDE).astype(F32)
    small[...] = jnp.zeros_like(small)
    for made in loads:
        made.wait()

    def exchange(value, at):
        xch[at] = value
        made = links.start(xch.at[at], xrecv.at[at], sib)
        made.wait_recv()

    def norm(resid):
        centered = resid - jnp.mean(resid, axis=1, keepdims=True)
        scale = lax.rsqrt(jnp.mean(centered * centered, axis=1, keepdims=True) + NORM_EPSILON)
        return centered * scale, scale

    BAND = 64

    def bands(body):
        for at in range(0, ROWS, BAND):
            body(slice(at, at + BAND))

    def forward(n):
        rounded = s[n].astype(BF)
        rnd[n] = rounded
        kv[n, 0, :, :FEAT] = nn(rounded, wqkv[:, FEAT : 2 * FEAT]).astype(BF)
        kv[n, 0, :, FEAT:] = (nn(rounded, wqkv[:, 2 * FEAT :]) + bias_v).astype(BF)
        came = [None]
        for slot, peer in ((1, to_x), (2, z1), (3, diag)):
            came.append(links.start(kv.at[n, 0], kv.at[n, slot], peer))
        q = (nn(rounded, wqkv[:, :FEAT]) + bias_q).astype(BF)
        qs = (q.astype(F32) * 0.125).astype(BF)
        for h in range(HEADC):
            q4[n, h * ROWS : (h + 1) * ROWS, :] = jnp.where(lane_head == h, qs, jnp.zeros_like(qs))
        for slot in range(SLOTS):
            if slot:
                came[slot].wait_recv()
            scores[...] = nt(kv[n, slot, :, :FEAT], q4[n])
            for at in range(0, QROWS, CHUNK):
                cut = slice(at, at + CHUNK)
                part = scores[:, cut] + biases[slot]
                top = jnp.max(part, axis=0, keepdims=True)
                e = jnp.exp(part - top)
                mrow[slot : slot + 1, cut] = top
                lrow[slot : slot + 1, cut] = colsum(e)
                probs[:, cut] = e.astype(BF)
            vt = kv[n, slot, :, FEAT:].T
            for h in range(HEADC):
                part_ctx[slot, h * 64 : (h + 1) * 64, :] = nn(
                    vt[h * 64 : (h + 1) * 64, :], probs[:, h * ROWS : (h + 1) * ROWS]
                )
        top = jnp.max(mrow[...], axis=0, keepdims=True)
        weight = jnp.exp(mrow[...] - top)
        total = jnp.sum(weight * lrow[...], axis=0, keepdims=True)
        logt[n] = top + jnp.log(total)
        weight = weight / total
        for h in range(HEADC):
            hr, hc = slice(h * 64, (h + 1) * 64), slice(h * ROWS, (h + 1) * ROWS)
            acc = part_ctx[0, hr, :] * weight[0:1, hc]
            for slot in range(1, SLOTS):
                acc = acc + part_ctx[slot, hr, :] * weight[slot : slot + 1, hc]
            ctxt[n, hr, :] = acc
        low = ctxt[n].astype(BF)
        ctxlt[n] = low
        exchange(tn(low, wout[...]), 2 * n)

        def first(band):
            resid = s[n, band, :] + (xch[2 * n, band, :] + xrecv[2 * n, band, :]) + row(2)
            hat, scale = norm(resid)
            x1[n, band, :] = hat
            rs1[n, band, :] = scale
            normed = hat * row(8) + row(10)
            gres[band, :] = normed
            n1low[n, band, :] = normed.astype(BF)

        bands(first)
        scores[...] = nn(n1low[n], wup[...]) + up_bias

        def act(band):
            v = scores[band, :]
            sq_v = v * v
            t = jnp.tanh(GELU_A * v * (1.0 + GELU_B * sq_v))
            half = 0.5 * (1.0 + t)
            hid[n, band, :] = (v * half).astype(BF)
            dgelu[n, band, :] = half + (0.5 * GELU_A) * v * (1.0 - t * t) * (
                1.0 + (3.0 * GELU_B) * sq_v
            )

        bands(act)
        exchange(nn(hid[n], wdown[...]), 2 * n + 1)

        def second(band):
            at = 2 * n + 1
            resid = gres[band, :] + (xch[at, band, :] + xrecv[at, band, :]) + row(7)
            hat, scale = norm(resid)
            x2[n, band, :] = hat
            rs2[n, band, :] = scale
            updated = hat * row(9) + row(11)
            s[n + 1, band, :] = jnp.where(caps[band, :] > n, updated, s[n, band, :])

        bands(second)

    for n in range(PONDER):
        forward(n)

    @pl.when(moved)
    def _():
        swaps[2].wait_recv()

    pair_ct = links.start(ct.at[c], ct.at[c], sib)
    pair_ct.wait_recv()
    halt = jax.nn.sigmoid(rowsum(s[0] * row(12)) + vec[13:14, 0:1])
    more = caps > 1.0
    mix_one = jnp.where(more, halt, 1.0)
    mix_two = jnp.where(more, 1.0 - halt, 0.0)
    fin_t[...] = mix_one * s[1] + mix_two * s[2]
    mine_rows = pl.ds(pl.multiple_of(c * TOK, TOK), TOK)
    fin_copy = links.copy(fin_t.at[mine_rows, :], final_out, swap)

    @pl.when(moved)
    def _():
        fin_copy.start()

    @pl.when(jnp.logical_not(moved))
    def _():
        final_out[...] = fin_t[mine_rows, :]

    cot = ct[...].reshape(ROWS, WIDE).astype(F32)
    grad_halt = jnp.where(
        more, rowsum(cot * s[1]) - rowsum(cot * s[2]) - PONDER_COST, 0.0
    )
    grad_logit = grad_halt * halt * (1.0 - halt)
    small[9:10, :] = colsum(grad_logit * s[0])
    small[10:11, :] = jnp.broadcast_to(colsum(grad_logit), (1, WIDE))

    def norm_back(grad, hat, scale, gain):
        g = grad * gain
        a = jnp.mean(g, axis=1, keepdims=True)
        b = jnp.mean(g * hat, axis=1, keepdims=True)
        return scale * (g - a - hat * b)

    def add_small(at, value):
        small[at : at + 1, : value.shape[1]] += value

    def add_grad(ref, value, first_time):
        value = value.reshape(ref.shape)
        if first_time:
            ref[...] = value
        else:
            ref[...] += value

    def backward(n, last):
        def two(band):
            active = caps[band, :] > n
            grad = jnp.where(active, gcur[band, :], 0.0)
            hat = x2[n, band, :]
            back = norm_back(grad, hat, rs2[n, band, :], row(9))
            gres[band, :] = back
            add_small(6, colsum(grad * hat))
            add_small(8, colsum(grad))
            rounded = back.astype(BF)
            add_small(4, colsum(rounded.astype(F32)))
            gmlp[band, :] = rounded
            gcur[band, :] = jnp.where(active, 0.0, gcur[band, :])

        gmlp = n1low.at[PONDER]
        bands(two)
        add_grad(gdown, tn(hid[n], gmlp[...]), last)
        scores[...] = nt(gmlp[...], wdown[...])

        def pre(band):
            grad = (dgelu[n, band, :] * scores[band, :]).astype(BF)
            probs[band, :] = grad
            total = colsum(grad.astype(F32))
            add_small(2, total[:, :WIDE])
            add_small(3, total[:, WIDE:])

        bands(pre)
        add_grad(gup, tn(n1low[n], probs[...]), last)
        at = 2 * PONDER + 2 * n
        exchange(nt(probs[...], wup[...]), at)

        def one(band):
            grad = gres[band, :] + (xch[at, band, :] + xrecv[at, band, :])
            hat = x1[n, band, :]
            back = norm_back(grad, hat, rs1[n, band, :], row(8))
            gres[band, :] = back
            add_small(5, colsum(grad * hat))
            add_small(7, colsum(grad))
            rounded = back.astype(BF)
            add_small(1, colsum(rounded.astype(F32)))
            gmlp[band, :] = rounded

        bands(one)
        add_grad(gout, nn(ctxlt[n], gmlp[...]), last)
        gctx = nt(gmlp[...], wout[...]).astype(BF)
        for h in range(HEADC):
            do4[h * ROWS : (h + 1) * ROWS, :] = jnp.where(lane_head == h, gctx, jnp.zeros_like(gctx))
        dots = nt(wout[...], gmlp[...]).astype(BF).astype(F32) * ctxt[n]
        for h in range(HEADC):
            drow[:, h * ROWS : (h + 1) * ROWS] = colsum(dots[h * 64 : (h + 1) * 64, :])
        came = [None] * SLOTS
        order = (3, 1, 2, 0)
        to = (None, to_x, z1, diag)
        for number, slot in enumerate(order):
            scores[...] = nt(kv[n, slot, :, :FEAT], q4[n])
            dprobs[...] = nt(kv[n, slot, :, FEAT:], do4[...])
            for cut_at in range(0, QROWS, CHUNK):
                cut = slice(cut_at, cut_at + CHUNK)
                p = jnp.exp(scores[:, cut] + biases[slot] - logt[n, :, cut])
                probs[:, cut] = p.astype(BF)
                dsc[:, cut] = (p * (dprobs[:, cut] - drow[:, cut])).astype(BF)
            dk = nn(dsc[...], q4[n])
            dv = nn(probs[...], do4[...])
            if slot:
                dkv_send[n, slot - 1, :, :FEAT] = dk.astype(BF)
                dkv_send[n, slot - 1, :, FEAT:] = dv.astype(BF)
                came[slot] = links.start(
                    dkv_send.at[n, slot - 1], dkv_recv.at[n, slot - 1], to[slot]
                )
            else:
                dkv_own[:, :FEAT] = dk
                dkv_own[:, FEAT:] = dv
            kt = kv[n, slot, :, :FEAT].T
            for h in range(HEADC):
                hr = slice(h * 64, (h + 1) * 64)
                term = nn(kt[hr, :], dsc[:, h * ROWS : (h + 1) * ROWS])
                if number == 0:
                    dqt[hr, :] = term
                else:
                    dqt[hr, :] += term
        dqkv[:, :FEAT] = (dqt[...] * 0.125).T.astype(BF)
        for slot in range(1, SLOTS):
            came[slot].wait_recv()
        dqkv[:, FEAT:] = (
            dkv_own[...]
            + dkv_recv[n, 0].astype(F32)
            + dkv_recv[n, 1].astype(F32)
            + dkv_recv[n, 2].astype(F32)
        ).astype(BF)
        add_small(0, jnp.concatenate(
            [colsum(dqkv[:, :FEAT].astype(F32)), colsum(dqkv[:, 2 * FEAT :].astype(F32))], axis=1
        ))
        at = 2 * PONDER + 2 * n + 1
        exchange(nt(dqkv[...], wqkv[...]), at)
        add_grad(gqkv, tn(rnd[n], dqkv[...]), last)

        def prev(band):
            gcur[band, :] = gcur[band, :] + gres[band, :] + (xch[at, band, :] + xrecv[at, band, :])

        bands(prev)

    gcur[...] = cot * mix_two
    backward(1, True)
    gcur[...] = gcur[...] + cot * mix_one
    backward(0, False)
    ig_t[...] = gcur[...] + grad_logit * row(12)
    ig_copy = links.copy(ig_t.at[mine_rows, :], igrad_out, swap)

    @pl.when(moved)
    def _():
        ig_copy.start()

    @pl.when(jnp.logical_not(moved))
    def _():
        igrad_out[...] = ig_t[mine_rows, :]

    grads = (gup, gdown, gqkv, gout)
    jobs = []
    for at, ref in enumerate(grads):
        quarter, width = ref.shape[2], ref.shape[3]
        jobs.append((ref, quarter, width, width // 2, sa_all[at], ra_all[at], sb_all[at], rb_all[at],
                     sc_all[at], rc_all[at], u_all[at], out_all[at]))
    stage_one, stage_two, stage_three = [], [], []
    small_one = links.start(small, smallx.at[0], to_x)
    for ref, quarter, width, half, sa, ra, sb, rb, sc, rc, u, out in jobs:
        sa[0] = ref[1 - x, :, :, :half].astype(BF)
        sa[1] = ref[:, 1 - y, :, half:].astype(BF)
        stage_one.append((links.start(sa.at[0], ra.at[0], to_x), links.start(sa.at[1], ra.at[1], to_y)))
    small_one.wait_recv()
    smallx[1] = small[...] + smallx[0]
    small_two = links.start(smallx.at[1], smallx.at[2], to_y)
    for (ref, quarter, width, half, sa, ra, sb, rb, sc, rc, u, out), (ca, cb) in zip(jobs, stage_one):
        ca.wait_recv()
        sb[0] = (ref[x, 1 - y, :, :half] + ra[0, 1 - y].astype(F32)).astype(BF)
        cb.wait_recv()
        sb[1] = (ref[1 - x, y, :, half:] + ra[1, 1 - x].astype(F32)).astype(BF)
        stage_two.append((links.start(sb.at[0], rb.at[0], to_y), links.start(sb.at[1], rb.at[1], to_x)))
    small_two.wait_recv()
    smallx[3] = smallx[1] + smallx[2]
    smallx[4 + z] = smallx[3]
    zs = (z1, z2, z3)
    small_three = [links.start(smallx.at[3], smallx.at[4 + z], peer) for peer in zs]
    zpos = (flip(z, 1), flip(z, 2), flip(flip(z, 1), 2))
    for (ref, quarter, width, half, sa, ra, sb, rb, sc, rc, u, out), (ca, cb) in zip(jobs, stage_two):
        ca.wait_recv()
        cb.wait_recv()
        u[:, :, :half] = (
            ref[x, y, :, :half] + ra[0, y].astype(F32) + rb[0].astype(F32)
        ).reshape(4, quarter // 4, half)
        u[:, :, half:] = (
            ref[x, y, :, half:] + ra[1, x].astype(F32) + rb[1].astype(F32)
        ).reshape(4, quarter // 4, half)
        copies = []
        for number, (peer, zp) in enumerate(zip(zs, zpos)):
            sc[number] = u[zp].astype(BF)
            copies.append(links.start(sc.at[number], rc.at[number], peer))
        stage_three.append(copies)
    for made in small_three:
        made.wait_recv()
    smallx[8 + c] = (smallx[4] + smallx[5]) + (smallx[6] + smallx[7])
    small_pair = links.start(smallx.at[8 + c], smallx.at[8 + c], sib)
    gather_z = []
    for (ref, quarter, width, half, sa, ra, sb, rb, sc, rc, u, out), copies in zip(jobs, stage_three):
        for made in copies:
            made.wait_recv()
        out[x, y, z] = (
            u[z] + rc[0].astype(F32) + rc[1].astype(F32) + rc[2].astype(F32)
        ).astype(BF)
        gather_z.append([links.start(out.at[x, y, z], out.at[x, y, z], peer) for peer in zs])
    gather_one = []
    for (ref, quarter, width, half, sa, ra, sb, rb, sc, rc, u, out), copies in zip(jobs, gather_z):
        for made in copies:
            made.wait_recv()
        lo, hi = pl.ds(0, half), pl.ds(half, half)
        gather_one.append((
            links.start(out.at[x, y, :, :, lo], out.at[x, y, :, :, lo], to_y),
            links.start(out.at[x, y, :, :, hi], out.at[x, y, :, :, hi], to_x),
        ))
    gather_two = []
    for (ref, quarter, width, half, sa, ra, sb, rb, sc, rc, u, out), (ca, cb) in zip(jobs, gather_one):
        ca.wait_recv()
        cb.wait_recv()
        lo, hi = pl.ds(0, half), pl.ds(half, half)
        gather_two.append((
            links.start(out.at[x, :, :, :, lo], out.at[x, :, :, :, lo], to_x),
            links.start(out.at[:, y, :, :, hi], out.at[:, y, :, :, hi], to_y),
        ))
    stores = []
    pair_stores = []

    def store(src, dst):
        made = pltpu.make_async_copy(src, dst, local_sem.at[len(loads) + len(stores)])
        made.start()
        stores.append(made)
        pair_stores.append(links.start(src, dst, sib))

    for at, ((ref, quarter, width, half, sa, ra, sb, rb, sc, rc, u, out), (ca, cb)) in enumerate(zip(jobs, gather_two)):
        ca.wait_recv()
        cb.wait_recv()
        if at == 0:
            store(out, gup_out.at[:, :, :, :, pl.ds(wide_own, HALF)])
        elif at == 1:
            store(out, gdown_out.at[c])
        elif at == 2:
            for third in range(3):
                store(
                    out.at[:, :, :, :, pl.ds(third * FEAT, FEAT)],
                    gqkv_out.at[:, :, :, :, pl.ds(pl.multiple_of(third * WIDE + own, FEAT), FEAT)],
                )
        else:
            store(out, gout_out.at[c])
    small_pair.wait_recv()
    small_out[...] = smallx[8:10]
    for made in stores:
        made.wait()
    for made in pair_stores:
        made.wait_recv()
    links.drain()

    @pl.when(moved)
    def _():
        for made in swaps:
            made.wait_send()
        for made in (fin_copy, ig_copy):
            made.wait_recv()
            made.wait_send()


GRAD_SHAPES = ((WIDE, HALF), (HALF, WIDE), (WIDE, 3 * FEAT), (FEAT, WIDE))


def fused_scratch():
    v = pltpu.VMEM
    P2 = PONDER
    groups = lambda make: [make(r, k) for r, k in GRAD_SHAPES]
    return [
        pltpu.SemaphoreType.DMA((N_LINKS,)),
        pltpu.SemaphoreType.DMA((N_LINKS,)),
        pltpu.SemaphoreType.DMA((16,)),
        v((WIDE, 3 * FEAT), BF), v((FEAT, WIDE), BF), v((WIDE, HALF), BF), v((HALF, WIDE), BF),
        v((2, TOK, WIDE), BF), v((2, TOK, WIDE), BF), v((2, TOK, 128), F32),
        v((P2 + 1, ROWS, WIDE), F32), v((P2, ROWS, WIDE), BF), v((P2, QROWS, FEAT), BF),
        v((P2, SLOTS, KEYS, WIDE), BF), v((P2, FEAT, ROWS), F32), v((P2, FEAT, ROWS), BF),
        v((P2, ROWS, WIDE), F32), v((P2, ROWS, 1), F32), v((P2 + 1, ROWS, WIDE), BF),
        v((P2, ROWS, HALF), BF), v((P2, ROWS, HALF), F32), v((P2, ROWS, WIDE), F32),
        v((P2, ROWS, 1), F32), v((P2, 1, QROWS), F32),
        v((KEYS, QROWS), F32), v((KEYS, QROWS), F32), v((KEYS, QROWS), BF), v((KEYS, QROWS), BF),
        v((SLOTS, QROWS), F32), v((SLOTS, QROWS), F32), v((SLOTS, FEAT, ROWS), F32),
        v((1, QROWS), F32), v((QROWS, FEAT), BF),
        v((4 * P2, ROWS, WIDE), F32), v((4 * P2, ROWS, WIDE), F32), v((ROWS, WIDE), F32),
        v((ROWS, WIDE), F32), v((FEAT, ROWS), F32), v((KEYS, WIDE), F32),
        v((P2, 3, KEYS, WIDE), BF), v((P2, 3, KEYS, WIDE), BF), v((ROWS, 3 * FEAT), BF),
        v((16, WIDE), F32),
        v((2, 2, HALF // 4, WIDE), F32), v((2, 2, WIDE // 4, HALF), F32),
        v((2, 2, WIDE // 4, 3 * FEAT), F32), v((2, 2, FEAT // 4, WIDE), F32),
        groups(lambda r, k: v((2, 2, r // 4, k // 2), BF)),
        groups(lambda r, k: v((2, 2, r // 4, k // 2), BF)),
        groups(lambda r, k: v((2, r // 4, k // 2), BF)),
        groups(lambda r, k: v((2, r // 4, k // 2), BF)),
        groups(lambda r, k: v((3, r // 16, k), BF)),
        groups(lambda r, k: v((3, r // 16, k), BF)),
        groups(lambda r, k: v((4, r // 16, k), F32)),
        groups(lambda r, k: v((2, 2, 4, r // 16, k), BF)),
        v((10, 16, WIDE), F32), v((ROWS, WIDE), F32), v((ROWS, WIDE), F32),
    ]


def fused_local(
    states, w_qkv, qv_bias, output_weight, out_bias, w_up, up_bias, w_down, down_bias,
    norm_gain, norm_shift, halt_weight, halt_bias, cotangent, lengths, caps,
):
    vec = jnp.concatenate(
        [
            qv_bias, out_bias[None], up_bias.reshape(4, WIDE), down_bias[None], norm_gain, norm_shift,
            halt_weight[None], jnp.broadcast_to(halt_bias[None], (1, WIDE)),
            jnp.zeros((2, WIDE), F32),
        ],
        axis=0,
    )
    lane = lax.broadcasted_iota(jnp.int32, (TOK, 128), 1)
    aux = jnp.where(
        lane == 0, caps.reshape(TOK, 1), jnp.where(lane == 1, lengths.reshape(1, 1), 0)
    ).astype(F32)
    vm = pl.BlockSpec(memory_space=pltpu.VMEM)
    hbm = pl.BlockSpec(memory_space=pl.ANY)
    outs = pl.pallas_call(
        fused_kernel,
        out_shape=(
            jax.ShapeDtypeStruct((TOK, WIDE), F32),
            jax.ShapeDtypeStruct((TOK, WIDE), F32),
            jax.ShapeDtypeStruct((2, 16, WIDE), F32),
            jax.ShapeDtypeStruct((2, 2, 4, WIDE // 16, 3 * WIDE), BF),
            jax.ShapeDtypeStruct((2, 2, 2, 4, FEAT // 16, WIDE), BF),
            jax.ShapeDtypeStruct((2, 2, 4, WIDE // 16, 2 * HALF), BF),
            jax.ShapeDtypeStruct((2, 2, 2, 4, HALF // 16, WIDE), BF),
        ),
        in_specs=[vm] * 4 + [hbm] * 4,
        out_specs=[vm] * 3 + [hbm] * 4,
        scratch_shapes=fused_scratch(),
        compiler_params=pltpu.CompilerParams(
            collective_id=0, has_side_effects=True, vmem_limit_bytes=62 * 2**20
        ),
        name="ponder",
    )(states[0], cotangent[0], aux, vec, w_qkv, output_weight, w_up, w_down)
    final, igrad, small, gqkv, gout, gup, gdown = outs
    pick = small[0]
    both = lambda i: jnp.concatenate([small[0, i], small[1, i]], axis=-1)
    grad_qv = jnp.stack(
        [
            jnp.concatenate([small[0, 0, :FEAT], small[1, 0, :FEAT]]),
            jnp.concatenate([small[0, 0, FEAT:], small[1, 0, FEAT:]]),
        ]
    )
    return (
        final[None],
        igrad[None],
        gqkv.reshape(WIDE, 3 * WIDE).astype(F32),
        grad_qv,
        gout.reshape(WIDE, WIDE).astype(F32),
        pick[1],
        gup.reshape(WIDE, 2 * HALF).astype(F32),
        small[:, 2:4].reshape(2 * HALF),
        gdown.reshape(2 * HALF, WIDE).astype(F32),
        pick[4],
        pick[5:7],
        pick[7:9],
        pick[9],
        pick[10, :1],
    )


SPECS_IN = (
    P("dp", "seq", None),) + (P(),) * 12 + (P("dp", "seq", None), P("dp"), P("dp", "seq"))
SPECS_OUT = (P("dp", "seq", None),) * 2 + (P(),) * 12


def solution(mesh):
    square = mesh.shape["dp"] == 4 and mesh.shape["seq"] == 8

    def whole(*arrays):
        states, w_up = arrays[0], arrays[5]
        fits = square and states.shape == (4, 8 * TOK, WIDE) and w_up.shape == (WIDE, 2 * HALF)
        return jax.shard_map(
            fused_local if fits else local,
            mesh=mesh,
            in_specs=SPECS_IN,
            out_specs=SPECS_OUT,
            check_vma=False,
        )(*arrays)

    return whole
```

```python
import functools
import math

import jax
import jax.numpy as jnp
from jax import lax
from jax.experimental import pallas as pl
from jax.experimental.pallas import tpu as pltpu
from jax.sharding import PartitionSpec as P

HEADS = 8
PONDER = 2


PONDER_COST = 0.01
NORM_EPSILON = 1e-05
MASK_FILL = -1e30


def normalize(resid, gain, shift):
    centered = resid - jnp.mean(resid, axis=-1, keepdims=True)
    spread = jnp.mean(centered * centered, axis=-1, keepdims=True)
    return centered * lax.rsqrt(spread + NORM_EPSILON) * gain + shift


def halt_mix(halt_probs, caps):
    step_count = halt_probs.shape[-1] + 1
    remain = jnp.ones(caps.shape, halt_probs.dtype)
    leftover = jnp.zeros(caps.shape, halt_probs.dtype)
    columns = []
    for number in range(step_count):
        if number < step_count - 1:
            partial_weight = halt_probs[..., number] * remain
        else:
            partial_weight = jnp.zeros(caps.shape, halt_probs.dtype)
        column = jnp.where(
            caps > number + 1, partial_weight, jnp.where(caps == number + 1, remain, 0.0)
        )
        columns.append(column)
        leftover = jnp.where(caps == number + 1, remain, leftover)
        if number < step_count - 1:
            remain = remain * (1.0 - halt_probs[..., number])
    return (jnp.stack(columns, -1), leftover)


def block_of_heads(piece_rows, offset_rows, block_len, head_count):
    sliced = lax.dynamic_slice_in_dim(piece_rows, offset_rows, block_len, 1)
    return sliced.reshape(sliced.shape[0], block_len, head_count, sliced.shape[2] // head_count)


def key_mask(lengths, offset_rows, block_len):
    positions = offset_rows + jnp.arange(block_len, dtype=jnp.int32)
    return (positions[None, :] < lengths[:, None])[:, None, None, :]


def attend(queries, key_rows, value_rows, lengths, head_count):
    seq_count, shard_len, model_width = queries.shape
    head_size = model_width // head_count
    score_scale = head_size ** (-0.5)
    query_heads = queries.reshape(seq_count, shard_len, head_count, head_size)
    start_state = (
        jnp.full((seq_count, head_count, shard_len), MASK_FILL, jnp.float32),
        jnp.zeros((seq_count, head_count, shard_len), jnp.float32),
        jnp.zeros((seq_count, shard_len, head_count, head_size), jnp.float32),
    )
    key_piece = lax.all_gather(key_rows, "seq", axis=1, tiled=True)
    value_piece = lax.all_gather(value_rows, "seq", axis=1, tiled=True)
    row_count = key_piece.shape[1]
    block_len = math.gcd(row_count, 512)

    def one_block(block_index, inner):
        running_max, running_sum, weighted = inner
        offset_rows = block_index * block_len
        key_block = block_of_heads(key_piece, offset_rows, block_len, head_count)
        value_block = block_of_heads(value_piece, offset_rows, block_len, head_count)
        key_valid = key_mask(lengths, offset_rows, block_len)
        scores = (
            jnp.einsum(
                "sqhe,skhe->shqk", query_heads, key_block, preferred_element_type=jnp.float32
            )
            * score_scale
        )
        scores = jnp.where(key_valid, scores, MASK_FILL)
        new_max = jnp.maximum(running_max, jnp.max(scores, axis=-1))
        unnormed = jnp.where(key_valid, jnp.exp(scores - new_max[..., None]), 0.0)
        factor = jnp.exp(running_max - new_max)
        running_sum = running_sum * factor + jnp.sum(unnormed, axis=-1)
        update = jnp.einsum(
            "shqk,skhe->sqhe",
            unnormed.astype(jnp.bfloat16),
            value_block,
            preferred_element_type=jnp.float32,
        )
        weighted = weighted * jnp.transpose(factor, (0, 2, 1))[..., None] + update
        return (new_max, running_sum, weighted)

    running_max, running_sum, weighted = lax.fori_loop(
        0, row_count // block_len, one_block, start_state
    )
    context = (weighted / jnp.transpose(running_sum, (0, 2, 1))[..., None]).reshape(queries.shape)
    log_total = jnp.transpose(running_max + jnp.log(running_sum), (0, 2, 1))
    return (context, log_total)


def attend_back(
    queries, key_rows, value_rows, lengths, head_count, grad_context, context, log_total
):
    seq_count, shard_len, model_width = queries.shape
    head_size = model_width // head_count
    score_scale = head_size ** (-0.5)
    query_heads = queries.reshape(seq_count, shard_len, head_count, head_size)
    grad_heads = grad_context.reshape(seq_count, shard_len, head_count, head_size)
    row_dots = jnp.sum(
        grad_context.astype(jnp.float32).reshape(grad_heads.shape)
        * context.reshape(grad_heads.shape),
        axis=-1,
    )
    dots_heads = jnp.transpose(row_dots, (0, 2, 1))
    log_heads = jnp.transpose(log_total, (0, 2, 1))
    total_len = shard_len * lax.axis_size("seq")
    start_state = (
        jnp.zeros(query_heads.shape, jnp.float32),
        jnp.zeros((seq_count, total_len, model_width), jnp.float32),
        jnp.zeros((seq_count, total_len, model_width), jnp.float32),
    )
    key_piece = lax.all_gather(key_rows, "seq", axis=1, tiled=True)
    value_piece = lax.all_gather(value_rows, "seq", axis=1, tiled=True)
    row_count = key_piece.shape[1]
    block_len = math.gcd(row_count, 512)

    def one_block(block_index, inner):
        grad_query, grad_key_all, grad_value_all = inner
        offset_rows = block_index * block_len
        key_block = block_of_heads(key_piece, offset_rows, block_len, head_count)
        value_block = block_of_heads(value_piece, offset_rows, block_len, head_count)
        key_valid = key_mask(lengths, offset_rows, block_len)
        scores = (
            jnp.einsum(
                "sqhe,skhe->shqk", query_heads, key_block, preferred_element_type=jnp.float32
            )
            * score_scale
        )
        probs = jnp.where(key_valid, jnp.exp(scores - log_heads[..., None]), 0.0)
        grad_probs = jnp.einsum(
            "sqhe,skhe->shqk", grad_heads, value_block, preferred_element_type=jnp.float32
        )
        grad_scores = (probs * (grad_probs - dots_heads[..., None])).astype(jnp.bfloat16)
        grad_query = grad_query + score_scale * jnp.einsum(
            "shqk,skhe->sqhe", grad_scores, key_block, preferred_element_type=jnp.float32
        )
        key_part = score_scale * jnp.einsum(
            "shqk,sqhe->skhe", grad_scores, query_heads, preferred_element_type=jnp.float32
        )
        value_part = jnp.einsum(
            "shqk,sqhe->skhe",
            probs.astype(jnp.bfloat16),
            grad_heads,
            preferred_element_type=jnp.float32,
        )
        grad_key_all = lax.dynamic_update_slice_in_dim(
            grad_key_all, key_part.reshape(seq_count, block_len, model_width), offset_rows, 1
        )
        grad_value_all = lax.dynamic_update_slice_in_dim(
            grad_value_all, value_part.reshape(seq_count, block_len, model_width), offset_rows, 1
        )
        return (grad_query, grad_key_all, grad_value_all)

    grad_query, grad_key_all, grad_value_all = lax.fori_loop(
        0, row_count // block_len, one_block, start_state
    )
    grad_key, grad_value = (
        lax.psum_scatter(grad_key_all, "seq", scatter_dimension=1, tiled=True),
        lax.psum_scatter(grad_value_all, "seq", scatter_dimension=1, tiled=True),
    )
    return (grad_query.reshape(queries.shape), grad_key, grad_value)


def forward_block(current, weights_tuple, lengths, head_count):
    (
        w_qkv,
        qv_bias,
        output_weight,
        out_bias,
        w_up,
        up_bias,
        w_down,
        down_bias,
        norm_gain,
        norm_shift,
    ) = weights_tuple
    model_width = current.shape[-1]
    rounded = current.astype(jnp.bfloat16)
    projected = jnp.einsum("snd,df->snf", rounded, w_qkv, preferred_element_type=jnp.float32)
    queries = (projected[..., :model_width] + qv_bias[0]).astype(jnp.bfloat16)
    key_rows = projected[..., model_width : 2 * model_width].astype(jnp.bfloat16)
    value_rows = (projected[..., 2 * model_width :] + qv_bias[1]).astype(jnp.bfloat16)
    context, log_total = attend(queries, key_rows, value_rows, lengths, head_count)
    context_reduced = context.astype(jnp.bfloat16)
    resid_one = (
        current
        + jnp.einsum(
            "jry,ym->jrm", context_reduced, output_weight, preferred_element_type=jnp.float32
        )
        + out_bias
    )
    normed_one = normalize(resid_one, norm_gain[0], norm_shift[0])
    normed_low = normed_one.astype(jnp.bfloat16)
    pre_hidden = (
        jnp.einsum("snd,df->snf", normed_low, w_up, preferred_element_type=jnp.float32) + up_bias
    )
    hidden_low = jax.nn.gelu(pre_hidden).astype(jnp.bfloat16)
    resid_two = (
        normed_one
        + jnp.einsum("snf,fd->snd", hidden_low, w_down, preferred_element_type=jnp.float32)
        + down_bias
    )
    updated = normalize(resid_two, norm_gain[1], norm_shift[1])
    return {
        "rounded": rounded,
        "queries": queries,
        "key_rows": key_rows,
        "value_rows": value_rows,
        "context": context,
        "log_total": log_total,
        "context_low": context_reduced,
        "resid_one": resid_one,
        "normed_low": normed_low,
        "pre_hidden": pre_hidden,
        "hidden_low": hidden_low,
        "resid_two": resid_two,
        "updated": updated,
    }


def backward_block(grad_updated, saved_entry, weights_tuple, lengths, head_count):
    (
        w_qkv,
        qv_bias,
        output_weight,
        out_bias,
        w_up,
        up_bias,
        w_down,
        down_bias,
        norm_gain,
        norm_shift,
    ) = weights_tuple
    model_width = output_weight.shape[0]
    _, pull_two = jax.vjp(normalize, saved_entry["resid_two"], norm_gain[1], norm_shift[1])
    grad_resid_two, gain_two, shift_two = pull_two(grad_updated)
    grad_mlp = grad_resid_two.astype(jnp.bfloat16)
    grad_down_bias = jnp.sum(grad_mlp.astype(jnp.float32), axis=(0, 1))
    grad_w_down = jnp.einsum(
        "snf,snd->fd", saved_entry["hidden_low"], grad_mlp, preferred_element_type=jnp.float32
    )
    grad_hidden = jnp.einsum("snd,fd->snf", grad_mlp, w_down, preferred_element_type=jnp.float32)
    _, pull_gelu = jax.vjp(jax.nn.gelu, saved_entry["pre_hidden"])
    grad_pre = pull_gelu(grad_hidden)[0].astype(jnp.bfloat16)
    grad_up_bias = jnp.sum(grad_pre.astype(jnp.float32), axis=(0, 1))
    grad_w_up = jnp.einsum(
        "snd,snf->df", saved_entry["normed_low"], grad_pre, preferred_element_type=jnp.float32
    )
    grad_normed = grad_resid_two + jnp.einsum(
        "snf,df->snd", grad_pre, w_up, preferred_element_type=jnp.float32
    )
    _, pull_one = jax.vjp(normalize, saved_entry["resid_one"], norm_gain[0], norm_shift[0])
    grad_resid_one, gain_one, shift_one = pull_one(grad_normed)
    attended_gradient = grad_resid_one.astype(jnp.bfloat16)
    grad_out_bias = jnp.sum(attended_gradient.astype(jnp.float32), axis=(0, 1))
    grad_w_out = jnp.einsum(
        "jhv,jhp->vp",
        saved_entry["context_low"],
        attended_gradient,
        preferred_element_type=jnp.float32,
    )
    grad_context = jnp.einsum(
        "yjo,io->yji", attended_gradient, output_weight, preferred_element_type=jnp.float32
    ).astype(jnp.bfloat16)
    grad_query, grad_key, grad_value = attend_back(
        saved_entry["queries"],
        saved_entry["key_rows"],
        saved_entry["value_rows"],
        lengths,
        head_count,
        grad_context,
        saved_entry["context"],
        saved_entry["log_total"],
    )
    grad_mixed = jnp.concatenate(
        [
            grad_query.astype(jnp.bfloat16),
            grad_key.astype(jnp.bfloat16),
            grad_value.astype(jnp.bfloat16),
        ],
        axis=-1,
    )
    grad_qv_bias = jnp.stack(
        [
            jnp.sum(grad_mixed[..., :model_width].astype(jnp.float32), axis=(0, 1)),
            jnp.sum(grad_mixed[..., 2 * model_width :].astype(jnp.float32), axis=(0, 1)),
        ]
    )
    grad_w_qkv = jnp.einsum(
        "snd,snf->df", saved_entry["rounded"], grad_mixed, preferred_element_type=jnp.float32
    )
    grad_current = grad_resid_one + jnp.einsum(
        "snf,df->snd", grad_mixed, w_qkv, preferred_element_type=jnp.float32
    )
    return (
        grad_current,
        (
            grad_w_qkv,
            grad_qv_bias,
            grad_w_out,
            grad_out_bias,
            grad_w_up,
            grad_up_bias,
            grad_w_down,
            grad_down_bias,
            jnp.stack([gain_one, gain_two]),
            jnp.stack([shift_one, shift_two]),
        ),
    )


def local(
    states,
    w_qkv,
    qv_bias,
    output_weight,
    out_bias,
    w_up,
    up_bias,
    w_down,
    down_bias,
    norm_gain,
    norm_shift,
    halt_weight,
    halt_bias,
    cotangent,
    lengths,
    caps,
):
    weights_tuple = (
        w_qkv,
        qv_bias,
        output_weight,
        out_bias,
        w_up,
        up_bias,
        w_down,
        down_bias,
        norm_gain,
        norm_shift,
    )
    head_count = HEADS
    current = states.astype(jnp.float32)
    inputs = []
    history = []
    prob_list = []
    for number in range(PONDER):
        if number < PONDER - 1:
            prob_list.append(jax.nn.sigmoid(jnp.sum(current * halt_weight, axis=-1) + halt_bias[0]))
        saved_entry = forward_block(current, weights_tuple, lengths, head_count)
        inputs.append(current)
        current = jnp.where((caps > number)[..., None], saved_entry["updated"], current)
        history.append(current)
    halt_probs = jnp.stack(prob_list, -1)
    (mixing, leftover), pull_halt = jax.vjp(lambda probs_in: halt_mix(probs_in, caps), halt_probs)
    final_state = jnp.zeros_like(current)
    for number in range(PONDER):
        final_state = final_state + mixing[..., number, None] * history[number]
    out_grad = cotangent.astype(jnp.float32)
    grad_mixing = jnp.stack(
        [jnp.sum(out_grad * history[number], axis=-1) for number in range(PONDER)], -1
    )
    grad_probs = pull_halt((grad_mixing, jnp.full(leftover.shape, PONDER_COST, jnp.float32)))[0]
    logits_gradient = grad_probs * halt_probs * (1.0 - halt_probs)
    totals = None
    grad_halt_weight = jnp.zeros(halt_weight.shape, jnp.float32)
    grad_halt_bias = jnp.zeros(halt_bias.shape, jnp.float32)
    grad_state = jnp.zeros(current.shape, jnp.float32)
    for number in reversed(range(PONDER)):
        grad_state = grad_state + out_grad * mixing[..., number, None]
        active = (caps > number)[..., None]
        grad_updated = jnp.where(active, grad_state, 0.0)
        passed = jnp.where(active, 0.0, grad_state)
        saved_entry = forward_block(inputs[number], weights_tuple, lengths, head_count)
        grad_prev, param_grads = backward_block(
            grad_updated, saved_entry, weights_tuple, lengths, head_count
        )
        totals = param_grads if totals is None else jax.tree.map(jnp.add, totals, param_grads)
        grad_state = passed + grad_prev
        if number < PONDER - 1:
            logit_grad = logits_gradient[..., number]
            grad_state = grad_state + logit_grad[..., None] * halt_weight
            grad_halt_weight = jnp.sum(logit_grad[..., None] * inputs[number], axis=(0, 1))
            grad_halt_bias = jnp.sum(logit_grad).reshape(1)
    summed = lax.psum(
        (
            totals[0],
            totals[1],
            totals[2],
            totals[3],
            totals[4],
            totals[5],
            totals[6],
            totals[7],
            totals[8],
            totals[9],
            grad_halt_weight,
            grad_halt_bias,
        ),
        ("dp", "seq"),
    )
    return (final_state, grad_state) + tuple(summed)


BF = jnp.bfloat16
F32 = jnp.float32
MESH = pl.DeviceIdType.MESH
GELU_A = math.sqrt(2.0 / math.pi)
GELU_B = 0.044715
TOK = 128
ROWS = 256
WIDE = 512
HALF = 1024
FEAT = 256
HEADC = 4
BLOCKS = 4
PAIR = 2
SEQ = BLOCKS * ROWS
QROWS = HEADC * ROWS
CHUNK = 128
BAND = 64
SAVED = BLOCKS + PAIR
HEAD = FEAT // HEADC

UNITS = ((64, 128),) * 8 + ((32, 256),) * 3 + ((16, 512),)
PLAN = (
    ("xy2", "y12x"),
    ("2D", "12D"),
    ("D2", "ZD"),
    ("2D", "DZ"),
    ("xy2", "x21y"),
    ("y2x", "21D"),
    ("D2", "21xy"),
    ("y2x", "21yx"),
    ("yx2", "DZ"),
    ("xy2", "ZD"),
    ("D2", "2D1"),
    ("yx2", "ZD"),
)
FIRST, SECOND = range(8), range(8, 12)
EVENTS = (
    (),
    (),
    (),
    (),
    (0, 5,),
    (1, 2,),
    (4, 7,),
    (),
    (3, 6, 0,),
    (5, 1,),
    (2, 4,),
    (7,),
    (3, 0, 5, 1,),
    (6,),
    (7,),
    (2, 0, 4,),
    (5, 3,),
    (),
    (1, 6,),
    (7, 0,),
    (5, 4,),
    (2,),
    (),
    (),
    (1, 6, 7, 3, 5, 8, 9, 0, 4, 10, 11, 6, 8, 7, 9, 4, 0, 11, 10, 6, 8, 9, 7, 11, 4, 10, 8, 9, 11, 10, 9, 8, 10, 11,),
)


def axes_of(stage):
    return {"D": "xy", "Z": "12"}.get(stage, stage)


def nn(a, b):
    return lax.dot_general(a, b, (((1,), (0,)), ((), ())), preferred_element_type=F32)


def nt(a, b):
    return lax.dot_general(a, b, (((1,), (1,)), ((), ())), preferred_element_type=F32)


def tn(a, b):
    return lax.dot_general(a, b, (((0,), (0,)), ((), ())), preferred_element_type=F32)


def colsum(v):
    return jnp.sum(v, axis=0, keepdims=True)


def rowsum(v):
    return jnp.sum(v, axis=1, keepdims=True)


class Links:
    def __init__(self, send, recv):
        self.send, self.recv, self.used, self.open = send, recv, 0, []

    def take(self, count):
        at = self.used
        self.used += count
        return at

    def copy(self, src, dst, device, at):
        return pltpu.make_async_remote_copy(
            src_ref=src,
            dst_ref=dst,
            send_sem=self.send.at[at],
            recv_sem=self.recv.at[at],
            device_id=device,
            device_id_type=MESH,
        )

    def start(self, src, dst, device):
        made = self.copy(src, dst, device, self.take(1))
        made.start()
        self.open.append(made)
        return made

    def drain(self):
        for made in self.open:
            made.wait_send()
        self.open = []


N_LINKS = 256


def each(low, high, body):
    def step(i, carry):
        body(i)
        return carry

    lax.fori_loop(low, high, step, 0)


def fused_kernel(
    states, cot_in, caps_in, length_in, qv_bias, out_bias, up_bias, down_bias, gains, shifts, halt_w, halt_b,
    wqkv_all, wout_all, wup_all, wdown_all,
    final_out, igrad_out, small_out, gqkv_out, gout_out, gup_out, gdown_out,
    send_sem, recv_sem, local_sem,
    wqkv, wout, wup, wdown,
    stg, ct, ax, bias, rnd, s, kk, vv, kt, vt, qq, q4, do4,
    big, pb, logt, ctxt, ctxlt, x1, x2, rs1, rs2, n1low, hid, dgelu,
    xs, xr, g, gmlp, gpre, dk, dv, dqt, drow, dqkv,
    mix, glog, acc, small, smallx, ig_s, ig_r,
    grads, sends, recvs, outs,
):
    dp = lax.axis_index("dp")
    sq = lax.axis_index("seq")
    x, y = lax.rem(dp, 2), dp // 2
    z, c = sq // 2, lax.rem(sq, 2)
    lo, hi = lax.rem(z, 2), z // 2

    def flip(value, bit):
        return value + bit - 2 * bit * lax.rem(value // bit, 2)

    sib = (dp, flip(sq, 1))
    to = {
        "x": (flip(dp, 1), sq),
        "y": (flip(dp, 2), sq),
        "1": (dp, flip(sq, 2)),
        "2": (dp, flip(sq, 4)),
    }
    far = (dp, flip(flip(sq, 2), 4))
    across = (flip(flip(dp, 1), 2), sq)
    peers = (sib, to["x"], to["y"], across, to["1"], to["2"], far)

    loads = []

    def load(src, dst):
        made = pltpu.make_async_copy(src, dst, local_sem.at[len(loads)])
        made.start()
        loads.append(made)

    own = pl.multiple_of(c * FEAT, FEAT)
    wide_own = pl.multiple_of(c * HALF, HALF)
    for third in range(3):
        load(
            wqkv_all.at[:, pl.ds(pl.multiple_of(third * WIDE + own, FEAT), FEAT)],
            wqkv.at[:, pl.ds(third * FEAT, FEAT)],
        )
    load(wout_all.at[pl.ds(own, FEAT), :], wout)
    load(wup_all.at[:, pl.ds(wide_own, HALF)], wup)
    load(wdown_all.at[pl.ds(wide_own, HALF), :], wdown)

    barrier = pltpu.get_barrier_semaphore()
    for peer in peers:
        pl.semaphore_signal(barrier, inc=1, device_id=peer, device_id_type=MESH)
    pl.semaphore_wait(barrier, len(peers))
    links = Links(send_sem, recv_sem)

    here = stg.at[z, c]
    others = (to["1"], to["2"], far)
    places = (flip(z, 1), flip(z, 2), flip(flip(z, 1), 2))
    came = [links.start(states, here, peer) for peer in others]
    beside = [links.start(states, here, sib)]
    stg[z, c] = states[...]

    row = lambda ref, i: ref[i : i + 1, :]
    flat = lambda ref: ref[...].reshape(1, -1)
    mine = lambda v: jnp.where(c == 0, v[:, :FEAT], v[:, FEAT:])
    b_q, b_v = mine(row(qv_bias, 0)), mine(row(qv_bias, 1))
    up_all = flat(up_bias)
    b_up = jnp.where(c == 0, up_all[:, :HALF], up_all[:, HALF:])
    b_out, b_down, w_halt = flat(out_bias), flat(down_bias), flat(halt_w)
    lane_head = lax.broadcasted_iota(jnp.int32, (1, FEAT), 1) // HEAD
    key_at = lax.broadcasted_iota(jnp.int32, (SEQ, ROWS), 0)
    bias[...] = jnp.where(key_at < length_in[0], 0.0, MASK_FILL)
    caps_row = caps_in[...].astype(F32)
    ax[lo, c] = jnp.broadcast_to(caps_row, (TOK, 128)).T
    acc[...] = jnp.zeros_like(acc)
    small[...] = jnp.zeros_like(small)
    for made in loads:
        made.wait()

    def block(ref, b):
        return ref[b].reshape(ROWS, WIDE)

    def queries(n, at, rounded):
        q = (nn(rounded, wqkv[:, :FEAT]) + b_q).astype(BF)
        qq[at] = (q.astype(F32) * 0.125).astype(BF)

    def keys(n, b, rounded):
        kk[n, b] = nn(rounded, wqkv[:, FEAT : 2 * FEAT]).astype(BF)
        value = (nn(rounded, wqkv[:, 2 * FEAT :]) + b_v).astype(BF)
        vv[n, b] = value
        vt[:, pl.ds(pl.multiple_of(b * ROWS, ROWS), ROWS)] = value.T

    beside[0].wait_recv()
    queries(0, z, block(stg, z))
    keys(0, z, block(stg, z))
    for made, place in zip(came, places):
        made.wait_recv()
        beside.append(links.start(stg.at[place, c], stg.at[place, c], sib))
    for made, place in zip(beside[1:], places):
        made.wait_recv()
        queries(0, place, block(stg, place))
        keys(0, place, block(stg, place))

    links_pair = []
    for src, ref in ((cot_in, ct), (ax.at[lo, c], ax)):
        links_pair.append((ref, links.start(src, ref.at[lo, c], to["1"]), links.start(src, ref.at[lo, c], sib)))
    ct[lo, c] = cot_in[...]

    def stack_heads(ref, value):
        for h in range(HEADC):
            ref[h * ROWS : (h + 1) * ROWS, :] = jnp.where(lane_head == h, value, jnp.zeros_like(value))

    def attention(n, at):
        stack_heads(q4, qq[at])
        key_all = kk[n].reshape(SEQ, FEAT)
        heads = [slice(h * ROWS, (h + 1) * ROWS) for h in range(HEADC)]

        def head_scores(h):
            big[:, heads[h % 2]] = nt(key_all, q4[heads[h], :])

        head_scores(0)
        for h, cut in enumerate(heads):
            buf = heads[h % 2]
            if h + 1 < HEADC:
                head_scores(h + 1)
            top = None
            for b in range(BLOCKS):
                r = slice(b * ROWS, (b + 1) * ROWS)
                m = jnp.max(big[r, buf] + bias[r, :], axis=0, keepdims=True)
                top = m if top is None else jnp.maximum(top, m)
            total = None
            for b in range(BLOCKS):
                r = slice(b * ROWS, (b + 1) * ROWS)
                e = jnp.exp(big[r, buf] + bias[r, :] - top)
                pb[r, buf] = e.astype(BF)
                total = colsum(e) if total is None else total + colsum(e)
            logt[at, :, cut] = top + jnp.log(total)
            hr = slice(h * HEAD, (h + 1) * HEAD)
            ctxt[at, hr, :] = nn(vt[hr, :], pb[:, buf]) * (1.0 / total)
        low = ctxt[at].astype(BF)
        ctxlt[:, pl.ds(pl.multiple_of(at * ROWS, ROWS), ROWS)] = low
        return tn(low, wout[...])

    SLOT_A, SLOT_M = 0, BLOCKS

    def swap_out(slot, i, first_sem, value):
        xs[slot + i] = value.astype(BF)
        links.copy(xs.at[slot + i], xr.at[slot + i], sib, first_sem + i).start()

    def swap_in(slot, i, first_sem):
        links.copy(xs.at[slot + i], xr.at[slot + i], sib, first_sem + i).wait()

    def swapped(slot, i, band):
        return xs[slot + i, band, :].astype(F32) + xr[slot + i, band, :].astype(F32)

    def norm(resid):
        centered = resid - jnp.mean(resid, axis=1, keepdims=True)
        scale = lax.rsqrt(jnp.mean(centered * centered, axis=1, keepdims=True) + NORM_EPSILON)
        return centered * scale, scale

    bands = [pl.ds(at, BAND) for at in range(0, ROWS, BAND)]
    cores = [(at // TOK, pl.ds(at % TOK, BAND)) for at in range(0, ROWS, BAND)]
    base = PAIR * hi

    def place_of(n, i):
        return i if n == 0 else base + i

    def saved_of(n, i):
        return i if n == 0 else BLOCKS + i

    def caps_of(i, part):
        return ax[i, part[0], part[1], 0:1]

    def forward(n):
        count = BLOCKS if n == 0 else PAIR
        sem_a, sem_m = links.take(count), links.take(count)
        each(0, count, lambda i: swap_out(SLOT_A, i, sem_a, attention(n, saved_of(n, i))))

        def middle(i):
            swap_in(SLOT_A, i, sem_a)
            at, place = saved_of(n, i), place_of(n, i)
            for band, part in zip(bands, cores):
                state = stg[place, part[0], part[1], :].astype(F32) if n == 0 else s[place, band, :]
                hat, scale = norm(state + swapped(SLOT_A, i, band) + b_out)
                x1[at, band, :] = hat
                rs1[at, band, :] = scale
                normed = hat * row(gains, 0) + row(shifts, 0)
                g[place, band, :] = normed
                n1low[at, band, :] = normed.astype(BF)
            for half in range(2):
                cols = slice(half * WIDE, (half + 1) * WIDE)
                big[half * ROWS : (half + 1) * ROWS, :] = nn(n1low[at], wup[:, cols]) + b_up[:, cols]
            for half in range(2):
                cols = slice(half * WIDE, (half + 1) * WIDE)
                for start in range(0, ROWS, BAND):
                    band = slice(start, start + BAND)
                    v = big[half * ROWS + start : half * ROWS + start + BAND, :]
                    v2 = v * v
                    t = jnp.tanh(GELU_A * v * (1.0 + GELU_B * v2))
                    up = 0.5 * (1.0 + t)
                    hid[at, band, cols] = (v * up).astype(BF)
                    dgelu[at, band, cols] = (
                        up + (0.5 * GELU_A) * v * (1.0 - t * t) * (1.0 + (3.0 * GELU_B) * v2)
                    ).astype(dgelu.dtype)
            swap_out(SLOT_M, i, sem_m, nn(hid[at], wdown[...]))

        each(0, count, middle)

        def last(i):
            swap_in(SLOT_M, i, sem_m)
            at, place = saved_of(n, i), place_of(n, i)
            for band, part in zip(bands, cores):
                hat, scale = norm(g[place, band, :] + swapped(SLOT_M, i, band) + b_down)
                x2[at, band, :] = hat
                rs2[at, band, :] = scale
                updated = hat * row(gains, 1) + row(shifts, 1)
                if n == 0:
                    s[place, band, :] = updated
                    rnd[place, band, :] = updated.astype(BF)
                else:
                    g[place, band, :] = jnp.where(caps_of(i, part) > n, updated, s[place, band, :])

        each(0, count, last)

    forward(0)
    for ref, from_pair, from_sib in links_pair:
        from_pair.wait_recv()
        from_sib.wait_recv()
    onward = [links.start(ref.at[1 - lo, c], ref.at[1 - lo, c], sib) for ref, _, _ in links_pair]
    each(0, BLOCKS, lambda b: keys(1, b, rnd[b]))
    each(0, PAIR, lambda i: queries(1, BLOCKS + i, rnd[base + i]))
    for made in onward:
        made.wait_recv()
    forward(1)

    mine_rows = pl.ds(pl.multiple_of(c * TOK, TOK), TOK)

    def halting(i):
        place = base + i
        first = stg[place].reshape(ROWS, WIDE).astype(F32)
        halt = jax.nn.sigmoid(rowsum(first * w_halt) + halt_b[0])
        more = ax[i].reshape(ROWS, 128)[:, 0:1] > 1.0
        mix[0, i] = jnp.where(more, halt, 1.0)
        mix[1, i] = jnp.where(more, 1.0 - halt, 0.0)
        cot = ct[i].reshape(ROWS, WIDE).astype(F32)
        through = jnp.where(more, rowsum(cot * s[place]) - rowsum(cot * g[place]) - PONDER_COST, 0.0)
        logit = through * halt * (1.0 - halt)
        glog[i] = logit
        acc[72:80, :] += jnp.sum((logit * first).reshape(ROWS // 8, 8, WIDE), axis=0)
        acc[80:81, :] += jnp.broadcast_to(colsum(logit), (1, WIDE))

    each(0, PAIR, halting)
    final_out[...] = mix[0, lo, mine_rows, :] * s[z, mine_rows, :] + mix[1, lo, mine_rows, :] * g[z, mine_rows, :]
    g[...] = jnp.zeros_like(g)

    def start_grad(i):
        g[base + i] = ct[i].reshape(ROWS, WIDE).astype(F32) * mix[1, i]

    each(0, PAIR, start_grad)

    def norm_back(grad, hat, scale, gain):
        v = grad * gain
        a = jnp.mean(v, axis=1, keepdims=True)
        b = jnp.mean(v * hat, axis=1, keepdims=True)
        return scale * (v - a - hat * b)

    def add_small(at, value, first_col=0):
        rows, width = value.shape
        cols = slice(first_col, first_col + width)
        acc[at * 8 : at * 8 + 8, cols] += jnp.sum(value.reshape(rows // 8, 8, width), axis=0)

    def add_unit(unit, value, fresh):
        ref = grads[unit]
        value = value.reshape(ref.shape)
        if fresh:
            ref[...] = value
        else:
            ref[...] += value

    half_cols = pl.ds(pl.multiple_of(lo * WIDE, WIDE), WIDE)

    def backward_mlp(n, fresh):
        count = BLOCKS if n == 0 else PAIR
        sem_a = links.take(count)
        first, end = (0, BLOCKS) if n == 0 else (BLOCKS, SAVED)

        def one(i):
            at, place = saved_of(n, i), place_of(n, i)
            for band, part in zip(bands, cores):
                grad = g[place, band, :]
                if n > 0:
                    grad = jnp.where(caps_of(i, part) > n, grad, 0.0)
                hat = x2[at, band, :]
                back = norm_back(grad, hat, rs2[at, band, :], row(gains, 1))
                g[place, band, :] = back
                add_small(6, grad * hat)
                add_small(8, grad)
                rounded = back.astype(BF)
                add_small(4, rounded.astype(F32))
                gmlp[i, band, :] = rounded
            for half in range(2):
                rows = slice(half * WIDE, (half + 1) * WIDE)
                big[half * ROWS : (half + 1) * ROWS, :] = nt(gmlp[i], wdown[rows, :])
            for half in range(2):
                cols = slice(half * WIDE, (half + 1) * WIDE)
                for start in range(0, ROWS, BAND):
                    band = slice(start, start + BAND)
                    above = big[half * ROWS + start : half * ROWS + start + BAND, :]
                    grad = (dgelu[at, band, cols].astype(F32) * above).astype(BF)
                    gpre[i, band, cols] = grad
                    add_small(2 + half, grad.astype(F32))
            swap_out(SLOT_A, i, sem_a, nt(gpre[i], wup[...]))

        each(0, count, one)
        length = count * ROWS
        down = tn(hid[first:end, :, half_cols].reshape(length, WIDE), gmlp[:count].reshape(length, WIDE))
        for k in range(4):
            add_unit(4 + k, down[:, k * 128 : (k + 1) * 128], fresh)
        up = tn(n1low[first:end].reshape(length, WIDE), gpre[:count, :, half_cols].reshape(length, WIDE))
        for k in range(4):
            add_unit(k, up[:, k * 128 : (k + 1) * 128], fresh)
        return sem_a

    def backward_norm(n, sem_a, beat=None):
        count = BLOCKS if n == 0 else PAIR

        def one(i):
            swap_in(SLOT_A, i, sem_a)
            at, place = saved_of(n, i), place_of(n, i)
            for band in bands:
                grad = g[place, band, :] + swapped(SLOT_A, i, band)
                hat = x1[at, band, :]
                back = norm_back(grad, hat, rs1[at, band, :], row(gains, 0))
                g[place, band, :] = back
                add_small(5, grad * hat)
                add_small(7, grad)
                rounded = back.astype(BF)
                add_small(1, rounded.astype(F32))
                gmlp[i, band, :] = rounded

        if beat is None:
            each(0, count, one)
        else:
            for i in range(count):
                one(i)
                beat()
        kt[...] = kk[n].reshape(SEQ, FEAT).T
        dk[...] = jnp.zeros_like(dk)
        dv[...] = jnp.zeros_like(dv)
        if n > 0:
            dqkv[:, :, :FEAT] = jnp.zeros((BLOCKS, ROWS, FEAT), BF)

    def backward_heads(n, i):
        at, place = saved_of(n, i), place_of(n, i)
        stack_heads(q4, qq[at])
        stack_heads(do4, nt(gmlp[i], wout[...]).astype(BF))
        dots = nt(wout[...], gmlp[i]).astype(BF).astype(F32) * ctxt[at]
        for h in range(HEADC):
            drow[:, h * ROWS : (h + 1) * ROWS] = colsum(dots[h * HEAD : (h + 1) * HEAD, :])

    span = SEQ // 2
    PARTS = 4

    def backward_part(n, i, part):
        at, place = saved_of(n, i), place_of(n, i)
        side, pair = part // 2, part % 2
        b0 = side * BLOCKS // 2
        keys_here = slice(b0, b0 + BLOCKS // 2)
        rows_here = slice(side * span, (side + 1) * span)
        cols = slice(pair * WIDE, (pair + 1) * WIDE)
        big[:span, :] = nt(kk[n, keys_here].reshape(span, FEAT), q4[cols, :])
        big[span:, :] = nt(vv[n, keys_here].reshape(span, FEAT), do4[cols, :])
        for cut_at in range(0, WIDE, CHUNK):
            cut = slice(cut_at, cut_at + CHUNK)
            q_cut = slice(pair * WIDE + cut_at, pair * WIDE + cut_at + CHUNK)
            for at_row in range(0, span, ROWS):
                r, r2 = slice(at_row, at_row + ROWS), slice(span + at_row, span + at_row + ROWS)
                key_rows = slice(side * span + at_row, side * span + at_row + ROWS)
                p = jnp.exp(big[r, cut] + bias[key_rows, :CHUNK] - logt[at, :, q_cut])
                pb[r, cut] = p.astype(BF)
                pb[r2, cut] = (p * (big[r2, cut] - drow[:, q_cut])).astype(BF)
        dv[rows_here, :] += nn(pb[:span, :], do4[cols, :])
        dk[rows_here, :] += nn(pb[span:, :], q4[cols, :])
        for h in range(2):
            head = 2 * pair + h
            hr = slice(head * HEAD, (head + 1) * HEAD)
            term = nn(kt[hr, rows_here], pb[span:, h * ROWS : (h + 1) * ROWS])
            if side == 0:
                dqt[hr, :] = term
            else:
                dqt[hr, :] += term
        if part == PARTS - 1:
            dqkv[place, :, :FEAT] = (dqt[...] * 0.125).T.astype(BF)

    def backward_attention(n, i):
        backward_heads(n, i)
        for part in range(PARTS):
            backward_part(n, i, part)

    def backward_rest(n, fresh, beat=None):
        count = BLOCKS if n == 0 else PAIR
        sem_m = links.take(BLOCKS)
        dqkv[:, :, FEAT : 2 * FEAT] = dk[...].reshape(BLOCKS, ROWS, FEAT).astype(BF)
        dqkv[:, :, 2 * FEAT :] = dv[...].reshape(BLOCKS, ROWS, FEAT).astype(BF)
        if beat is None:
            each(0, BLOCKS, lambda b: swap_out(SLOT_M, b, sem_m, nt(dqkv[b], wqkv[...])))
        else:
            for b in range(BLOCKS):
                swap_out(SLOT_M, b, sem_m, nt(dqkv[b], wqkv[...]))
                beat()
        length = count * ROWS
        at = 0 if n == 0 else SEQ
        side = ctxlt[pl.ds(pl.multiple_of(lo * TOK, TOK), TOK), at : at + length]
        add_unit(11, nn(side, gmlp[:count].reshape(length, WIDE)), fresh)
        grad = dqkv[...].reshape(SEQ, 3 * FEAT)
        add_small(0, grad[:, :FEAT].astype(F32))
        add_small(0, grad[:, 2 * FEAT :].astype(F32), FEAT)
        quarter = pl.ds(pl.multiple_of(lo * ROWS, ROWS), ROWS)
        source = stg[:, :, :, quarter] if n == 0 else rnd[:, :, quarter]
        total = tn(source.reshape(SEQ, ROWS), grad)
        for k in range(3):
            add_unit(8 + k, total[:, k * FEAT : (k + 1) * FEAT], fresh)
        return sem_m

    def backward_end(sem_m):
        def one(b):
            swap_in(SLOT_M, b, sem_m)
            for band in bands:
                g[b, band, :] += swapped(SLOT_M, b, band)

        each(0, BLOCKS, one)

    sem = backward_mlp(1, True)
    backward_norm(1, sem)
    each(0, PAIR, lambda i: backward_attention(1, i))
    backward_end(backward_rest(1, True))

    def add_first(i):
        cot = ct[i].reshape(ROWS, WIDE).astype(F32)
        active = ax[i].reshape(ROWS, 128)[:, 0:1] > 1.0
        passed = jnp.where(active, 0.0, cot * mix[1, i])
        g[base + i] = g[base + i] + passed + cot * mix[0, i]

    each(0, PAIR, add_first)

    place_on = {"x": x, "y": y, "1": lo, "2": hi}
    RS_DIMS, AG_DIMS = "2xy", "12xy"
    flip_of = {"x": (1, 0), "y": (2, 0), "1": (0, 2), "2": (0, 4)}

    def pick(dims, fixed):
        return tuple(fixed.get(d, slice(None)) for d in dims)

    def toward(dims):
        at_dp, at_sq = dp, sq
        for d in dims:
            one, two = flip_of[d]
            at_dp = flip(at_dp, one) if one else at_dp
            at_sq = flip(at_sq, two) if two else at_sq
        return (at_dp, at_sq)

    def subsets(dims):
        return [dims] if len(dims) == 1 else [dims[:1], dims[1:], dims]

    class Unit:
        def __init__(self, number):
            self.number = number
            reduce, gather = PLAN[number]
            self.count = len(reduce) + len(gather)
            self.stages = []
            fixed = {}
            left = {d: place_on[d] for d in AG_DIMS}
            for at, dims in enumerate(map(axes_of, reduce + gather)):
                reducing = at < len(reduce)
                copies, cuts = [], []
                for which, some in enumerate(subsets(dims)):
                    if reducing:
                        cut = dict(fixed)
                        for d in dims:
                            cut[d] = 1 - place_on[d] if d in some else place_on[d]
                        cuts.append(cut)
                        src, dst = sends[number][at][which], recvs[number][at][which]
                    else:
                        src = dst = outs[number].at[pick(AG_DIMS, left)]
                    copies.append((src, dst, toward(some), links.take(1)))
                for d in dims:
                    if reducing:
                        fixed[d] = place_on[d]
                    else:
                        del left[d]
                self.stages.append((reducing, copies, cuts, dict(fixed)))

        def launch(self, at):
            reducing, copies, cuts, _ = self.stages[at]
            for which, copy in enumerate(copies):
                if reducing:
                    copy[0][...] = grads[self.number][pick(RS_DIMS, cuts[which])].astype(BF)
                links.copy(*copy).start()

        def advance(self, at):
            n = self.number
            reducing, copies, _, fixed = self.stages[at]
            for copy in copies:
                links.copy(*copy).wait_recv()
            if reducing:
                keep = pick(RS_DIMS, fixed)
                total = grads[n][keep]
                for copy in copies:
                    total = total + copy[1][...].astype(F32)
                if len(fixed) < 3:
                    grads[n][keep] = total
                else:
                    outs[n][pick(AG_DIMS, place_on)] = total.astype(BF)
            if at + 1 < self.count:
                self.launch(at + 1)
            else:
                store_unit(n)

        def drain(self):
            for _, copies, _, _ in self.stages:
                for copy in copies:
                    links.copy(*copy).wait_send()

    stores = []
    pair_stores = []

    def store(src, dst):
        made = pltpu.make_async_copy(src, dst, local_sem.at[len(loads) + len(stores)])
        made.start()
        stores.append(made)
        pair_stores.append(links.start(src, dst, sib))

    def store_unit(n):
        if n < 4:
            store(outs[n], gup_out.at[c, n])
        elif n < 8:
            store(outs[n], gdown_out.at[c, n - 4])
        elif n < 11:
            store(outs[n], gqkv_out.at[c, n - 8])
        else:
            store(outs[n], gout_out.at[c])

    units = [Unit(number) for number in range(12)]

    steps, seen = [], [0] * len(units)
    for group in EVENTS:
        steps.append([])
        for number in group:
            steps[-1].append((number, seen[number]))
            seen[number] += 1

    def run(group):
        for number, at in steps[group]:
            units[number].advance(at)

    beats = [0]

    def beat():
        run(beats[0])
        beats[0] += 1

    sem = backward_mlp(0, False)
    for number in FIRST:
        units[number].launch(0)
    backward_norm(0, sem, beat)
    first_group = beats[0]

    def attention_round(i):
        backward_heads(0, i)
        for part in range(PARTS):
            backward_part(0, i, part)
            for turn in range(BLOCKS):
                group = first_group + turn * PARTS + part
                if steps[group]:
                    pl.when(i == turn)(functools.partial(run, group))

    each(0, BLOCKS, attention_round)
    beats[0] += BLOCKS * PARTS
    sem = backward_rest(0, False, beat)
    for number in SECOND:
        units[number].launch(0)
    backward_end(sem)

    def add_halt(i):
        g[base + i] = g[base + i] + glog[i] * w_halt

    each(0, PAIR, add_halt)
    ig_s[...] = g[flip(z, 2), mine_rows, :].astype(BF)
    ig_copy = links.start(ig_s, ig_r, to["2"])
    for at in range(11):
        small[at : at + 1, :] = colsum(acc[at * 8 : at * 8 + 8, :])
    small_now = small
    last = list(steps[beats[0]])
    for number, d in enumerate("xy2"):
        made = links.start(small_now, smallx.at[2 * number], to[d])
        for _ in range(6):
            unit, at = last.pop(0)
            units[unit].advance(at)
        made.wait_recv()
        smallx[2 * number + 1] = small_now[...] + smallx[2 * number]
        small_now = smallx.at[2 * number + 1]
    small_out[c] = small_now[...]
    small_pair = links.start(small_now, small_out.at[c], sib)
    ig_copy.wait_recv()
    igrad_out[...] = g[z, mine_rows, :] + ig_r[...].astype(F32)
    for unit, at in last:
        units[unit].advance(at)
    small_pair.wait_recv()
    for made in stores:
        made.wait()
    for made in pair_stores:
        made.wait_recv()
    for unit in units:
        unit.drain()
    links.drain()


def fused_scratch():
    v = pltpu.VMEM
    dma = pltpu.SemaphoreType.DMA
    f = lambda *shape: v(shape, F32)
    h = lambda *shape: v(shape, BF)
    grads = [f(2, 2, 2, r, k) for r, k in UNITS]

    def parts():
        made = []
        for (r, k), (reduce, _) in zip(UNITS, PLAN):
            left, stages = [2, 2, 2], []
            for dims in map(axes_of, reduce):
                left = left[len(dims) :]
                stages.append([h(*left, r, k) for _ in range(2 ** len(dims) - 1)])
            made.append(stages)
        return made

    return [
        dma((N_LINKS,)), dma((N_LINKS,)), dma((32,)),
        h(WIDE, 3 * FEAT), h(FEAT, WIDE), h(WIDE, HALF), h(HALF, WIDE),
        h(BLOCKS, 2, TOK, WIDE), h(PAIR, 2, TOK, WIDE), f(PAIR, 2, TOK, 128), f(SEQ, 256),
        h(BLOCKS, ROWS, WIDE), f(BLOCKS, ROWS, WIDE),
        h(2, BLOCKS, ROWS, FEAT), h(2, BLOCKS, ROWS, FEAT), h(FEAT, SEQ), h(FEAT, SEQ),
        h(SAVED, ROWS, FEAT), h(QROWS, FEAT), h(QROWS, FEAT),
        f(SEQ, WIDE), h(SEQ, WIDE), f(SAVED, 1, QROWS), f(SAVED, FEAT, ROWS), h(FEAT, SAVED * ROWS),
        f(SAVED, ROWS, WIDE), f(SAVED, ROWS, WIDE), f(SAVED, ROWS, 1), f(SAVED, ROWS, 1),
        h(SAVED, ROWS, WIDE), h(SAVED, ROWS, HALF), h(SAVED, ROWS, HALF),
        h(2 * BLOCKS, ROWS, WIDE), h(2 * BLOCKS, ROWS, WIDE),
        f(BLOCKS, ROWS, WIDE), h(BLOCKS, ROWS, WIDE), h(BLOCKS, ROWS, HALF),
        f(SEQ, FEAT), f(SEQ, FEAT), f(FEAT, ROWS), f(1, QROWS), h(BLOCKS, ROWS, 3 * FEAT),
        f(2, PAIR, ROWS, 1), f(PAIR, ROWS, 1), f(88, WIDE), f(16, WIDE), f(6, 16, WIDE), h(TOK, WIDE), h(TOK, WIDE),
        grads, parts(), parts(),
        [h(2, 2, 2, 2, r, k) for r, k in UNITS],
    ]


BIG = ((WIDE, 3 * WIDE), (WIDE, WIDE), (WIDE, 2 * HALF), (2 * HALF, WIDE))


def widen_kernel(gqkv, gout, gup, gdown, small, final, igrad,
                 o_final, o_igrad, o_qkv, o_qv, o_out, o_ob, o_up, o_ub, o_down, o_db, o_gain, o_shift, o_hw, o_hb,
                 narrow, wide, read_sem, write_sem):
    half = lambda at: BIG[at][0] // 2
    groups = []
    for core in range(2):
        rows = pl.ds(core * HALF, HALF)
        groups.append(([(gdown.at[core, k], narrow[3].at[rows, pl.ds(k * 128, 128)]) for k in range(4)],
                       [(3, rows)]))
    both = lambda at: [(at, pl.ds(0, half(at))), (at, pl.ds(half(at), half(at)))]
    groups.append(([(gup.at[core, k, b], narrow[2].at[:, pl.ds(core * HALF + b * WIDE + k * 128, 128)])
                    for core in range(2) for k in range(4) for b in range(2)], both(2)))
    groups.append(([(gqkv.at[core, k], narrow[0].at[:, pl.ds(k * WIDE + core * FEAT, FEAT)])
                    for core in range(2) for k in range(3)], both(0)))
    groups.append(([(gout, narrow[1])], [(1, pl.ds(0, WIDE))]))
    results = (o_qkv, o_out, o_up, o_down)
    reads, writes = [], []
    count = 0
    for sources, _ in groups:
        some = []
        for src, dst in sources:
            made = pltpu.make_async_copy(src, dst, read_sem.at[count])
            count += 1
            made.start()
            some.append(made)
        reads.append(some)
    for some, (_, pieces) in zip(reads, groups):
        for made in some:
            made.wait()
        for at, rows in pieces:
            wide[at][rows, :] = narrow[at][rows, :].astype(F32)
            made = pltpu.make_async_copy(wide[at].at[rows, :], results[at].at[rows, :], write_sem.at[len(writes)])
            made.start()
            writes.append(made)
    o_final[...] = final[...]
    o_igrad[...] = igrad[...]
    a, b = small[0], small[1]
    row = lambda v, i: v[i : i + 1, :]
    o_qv[0:1, :FEAT] = a[0:1, :FEAT]
    o_qv[0:1, FEAT:] = b[0:1, :FEAT]
    o_qv[1:2, :FEAT] = a[0:1, FEAT:]
    o_qv[1:2, FEAT:] = b[0:1, FEAT:]
    o_ob[...] = row(a, 1).reshape(WIDE)
    for k, v in enumerate((a, b)):
        for j in range(2):
            o_ub[pl.ds((2 * k + j) * WIDE, WIDE)] = row(v, 2 + j).reshape(WIDE)
    o_db[...] = row(a, 4).reshape(WIDE)
    o_gain[...] = a[5:7, :]
    o_shift[...] = a[7:9, :]
    o_hw[...] = row(a, 9).reshape(WIDE)
    o_hb[...] = row(a, 10)[:, :128].reshape(128)
    for made in writes:
        made.wait()


def widen(final, igrad, small, gqkv, gout, gup, gdown):
    shapes = [
        (TOK, WIDE), (TOK, WIDE), BIG[0], (2, WIDE), BIG[1], (WIDE,), BIG[2], (2 * HALF,), BIG[3], (WIDE,),
        (2, WIDE), (2, WIDE), (WIDE,), (128,),
    ]
    vm = pl.BlockSpec(memory_space=pltpu.VMEM)
    hbm = pl.BlockSpec(memory_space=pl.ANY)
    return pl.pallas_call(
        widen_kernel,
        out_shape=tuple(jax.ShapeDtypeStruct(a, F32) for a in shapes),
        in_specs=[hbm] * 4 + [vm] * 3,
        out_specs=tuple(hbm if a in BIG else vm for a in shapes),
        scratch_shapes=[
            [pltpu.VMEM(a, BF) for a in BIG],
            [pltpu.VMEM(a, F32) for a in BIG],
            pltpu.SemaphoreType.DMA((32,)),
            pltpu.SemaphoreType.DMA((8,)),
        ],
        compiler_params=pltpu.CompilerParams(vmem_limit_bytes=62 * 2**20),
        name="widen",
    )(gqkv.reshape(2, 3, WIDE, FEAT), gout.reshape(BIG[1]), gup.reshape(2, 4, 2, WIDE, 128),
      gdown.reshape(2, 4, HALF, 128), small, final, igrad)


def fused_local(
    states, w_qkv, qv_bias, output_weight, out_bias, w_up, up_bias, w_down, down_bias,
    norm_gain, norm_shift, halt_weight, halt_bias, cotangent, lengths, caps,
):
    vm = pl.BlockSpec(memory_space=pltpu.VMEM)
    sm = pl.BlockSpec(memory_space=pltpu.SMEM)
    hbm = pl.BlockSpec(memory_space=pl.ANY)
    out = lambda *shape: jax.ShapeDtypeStruct(shape, BF)
    made = pl.pallas_call(
        fused_kernel,
        out_shape=(
            jax.ShapeDtypeStruct((TOK, WIDE), F32),
            jax.ShapeDtypeStruct((TOK, WIDE), F32),
            jax.ShapeDtypeStruct((2, 16, WIDE), F32),
            out(2, 3, 2, 2, 2, 2, *UNITS[8]),
            out(2, 2, 2, 2, 2, *UNITS[11]),
            out(2, 4, 2, 2, 2, 2, *UNITS[0]),
            out(2, 4, 2, 2, 2, 2, *UNITS[4]),
        ),
        in_specs=[vm] * 3 + [sm] + [vm] * 7 + [sm] + [hbm] * 4,
        out_specs=[vm] * 3 + [hbm] * 4,
        scratch_shapes=fused_scratch(),
        compiler_params=pltpu.CompilerParams(
            collective_id=0, has_side_effects=True, vmem_limit_bytes=64 * 2**20 - 2**18
        ),
        name="ponder",
    )(states[0], cotangent[0], caps, lengths, qv_bias, out_bias, up_bias, down_bias, norm_gain, norm_shift,
      halt_weight, halt_bias, w_qkv, output_weight, w_up, w_down)
    final, igrad, gqkv, grad_qv, gout, g_ob, gup, g_ub, gdown, g_db, gain, shift, g_hw, g_hb = widen(*made)
    return (
        final[None], igrad[None], gqkv, grad_qv, gout, g_ob, gup, g_ub, gdown, g_db, gain, shift, g_hw, g_hb[:1]
    )


SPECS_IN = (P("dp", "seq", None),) + (P(),) * 12 + (P("dp", "seq", None), P("dp"), P("dp", "seq"))
SPECS_OUT = (P("dp", "seq", None),) * 2 + (P(),) * 12


def solution(mesh):
    square = mesh.shape["dp"] == 4 and mesh.shape["seq"] == 2 * BLOCKS

    def whole(*arrays):
        states, w_up = arrays[0], arrays[5]
        fits = square and states.shape == (4, SEQ, WIDE) and w_up.shape == (WIDE, 2 * HALF)
        return jax.shard_map(
            fused_local if fits else local,
            mesh=mesh,
            in_specs=SPECS_IN,
            out_specs=SPECS_OUT,
            check_vma=False,
        )(*arrays)

    return whole
```
